32 devices in a mesh: rep: 2 (over y), dp: 4 (over z), tensor: 4 (over x, core).
Axes of the slice: x: 2, y: 2, z: 4, core: 2. Of those that a mesh axis runs over, the one named last changes fastest.
Arguments:
- tokens: bfloat16 [4096, 4096], P(('rep', 'dp', 'tensor')), parts along dimension 0, may hold values from -6 to 6
- grad_out: bfloat16 [4096, 14336], P(('rep', 'dp'), 'tensor'), parts along dimension 0, may hold values from -6 to 6
- frozen_weight: bfloat16 [4096, 14336], P('dp', 'tensor'), may hold values from -0.09375 to 0.09375
- adapter_down: bfloat16 [128, 16, 4096], P('rep', None, 'tensor'), parts along dimension 0, may hold values from -0.09375 to 0.09375
- adapter_up: bfloat16 [128, 16, 14336], P('rep', None, 'tensor'), parts along dimension 0, may hold values from -0.1875 to 0.1875
- tenant_ids: int32 [4096], P('rep'), parts along dimension 0, may hold values from 0 to 63, as said below
- tenant_token_counts: int32 [128], P('rep'), parts along dimension 0, may hold values from 0 to 512, as said below
- owner_map: int32 [64], replicated, may hold values from 0 to 3, as said below
Outputs:
- input_grad: bfloat16 [4096, 4096], P(('rep', 'dp', 'tensor')), parts along dimension 0
- grad_down: float32 [256, 16, 4096], P(('rep', 'dp'), None, 'tensor'), parts along dimension 0
- grad_up: float32 [256, 16, 14336], P(('rep', 'dp'), None, 'tensor'), parts along dimension 0
The draws below stay inside these ranges and needn't reach their ends.
There are 2 independent parts, one for each index of `rep`. The reference program is written for one: setup_inputs(seed, part) draws one part's arguments, and reference() takes and returns one part's arrays. A program takes and returns all parts, laid end to end along the dimension named above; an argument that names none is the same for every part. Nothing has to cross between parts.
Inputs may be any that keep to these rules, and one draw needn't show every extreme that they name: `tenant_ids`: constant on aligned blocks of 128 rows; the 4 blocks of one data group name different tenants; some tenant has a block in every data group. `tenant_token_counts`: 128 times the number of blocks of tenant_ids that name the tenant. `owner_map`: no owner holds more than 32 adapters, and one holds exactly 32.
All inputs are finite; a program needn't handle non-finite values.
Results may differ from the reference program's by a relative error of at most 0.014.
Values may be sent and summed in bfloat16 or wider, within the bound.
No kernel may reach another device: no remote copies, remote signals or barrier semaphores. Data moves between devices by JAX's collectives and lax.ppermute only.
A program may use at most 192 MiB of HBM per device.

```python
import jax
import jax.numpy as jnp
from jax import lax

MODEL_WIDTH = 4096
FF = 14336
R = 16
ADAPTERS = 64
TILE = 128
GROUP_TOKENS = 512
TOKENS = 2048
TILES = 4
SLOTS = 32
OWNED = 128
N_DP = 4
N_TENSOR = 4


def pick_one_group(group_key, common):
    order_key, place_key = jax.random.split(group_key)
    others = jax.random.permutation(order_key, ADAPTERS - 1)[:TILES - 1].astype(jnp.int32)
    others = (others + (others >= common).astype(jnp.int32)).astype(jnp.int32)
    listed = jnp.concatenate([jnp.full((1,), common, jnp.int32), others])
    order = jax.random.permutation(place_key, TILES)
    return listed[order].astype(jnp.int32)


def tile_tenants(key):
    common_key, rest_key = jax.random.split(key)
    common = jax.random.randint(common_key, (), 0, ADAPTERS).astype(jnp.int32)
    group_keys = jax.random.split(rest_key, TOKENS // GROUP_TOKENS)
    selected_slot = jax.vmap(pick_one_group, in_axes=(0, None))(group_keys, common)
    return selected_slot.reshape(-1).astype(jnp.int32)


def draw_tenant_ids(key, part):
    selected_slot = tile_tenants(key)
    return jnp.repeat(selected_slot, TILE).astype(jnp.int32)


def draw_tenant_token_counts(key, part):
    selected_slot = tile_tenants(key)
    matches = (selected_slot[:, None] == jnp.arange(ADAPTERS)[None, :]).astype(jnp.int32)
    return (TILE * jnp.sum(matches, axis=0)).astype(jnp.int32)


def draw_owner_map(key, part):
    key = jax.random.fold_in(key, 7)
    first_key, second_key, third_key = jax.random.split(key, 3)
    owner_total = OWNED // SLOTS
    positions = jax.random.permutation(first_key, ADAPTERS)
    busiest = jax.random.randint(second_key, (), 0, owner_total).astype(jnp.int32)
    seat_owner = (jnp.arange((owner_total - 1) * SLOTS) // SLOTS).astype(jnp.int32)
    seat_owner = seat_owner + (seat_owner >= busiest).astype(jnp.int32)
    seat_owner = jax.random.permutation(third_key, seat_owner)
    assigned = jnp.concatenate([jnp.full((SLOTS,), busiest, jnp.int32), seat_owner[:ADAPTERS - SLOTS].astype(jnp.int32)])
    return jnp.zeros((ADAPTERS,), jnp.int32).at[positions].set(assigned)


def block_scale(key, extent, pieces, low, high):
    def one(dim, blocks):
        steps = jax.random.uniform(jax.random.fold_in(jax.random.fold_in(key, 6), dim), (blocks,), jnp.float32, low / len(pieces), high / len(pieces))
        return jnp.repeat(jnp.exp(steps), extent[dim] // blocks).reshape((-1,) + (1,) * (len(extent) - dim - 1))

    level = one(*pieces[0])
    for cut in pieces[1:]:
        level = level * one(*cut)
    return level


def scatter_about(own_key, extent, deviation, bound, pieces=(), kind=jnp.bfloat16):
    result = jax.random.normal(own_key, extent, jnp.float32) * deviation
    if len(pieces) > 0:
        result = block_scale(own_key, extent, pieces, -0.22, 0.18) * result
    return jnp.clip(result, min=-bound, max=bound).astype(kind)


def setup_inputs(seed: int = 0, part: int = 0) -> dict:
    key_list = jax.random.split(jax.random.key(seed), 9)
    part_splits = jax.random.split(jax.random.fold_in(key_list[8], part), 9)
    tokens = scatter_about(part_splits[0], (TOKENS, MODEL_WIDTH), 1.0, 6.0, ((0, 16),))
    grad_out = scatter_about(part_splits[1], (TOKENS, FF), 1.0, 6.0, ((0, 4), (1, 4)))
    frozen_weight = scatter_about(key_list[2], (MODEL_WIDTH, FF), MODEL_WIDTH ** -0.5, 0.09375, ((0, 4), (1, 4)))
    adapter_down = scatter_about(part_splits[3], (ADAPTERS, R, MODEL_WIDTH), MODEL_WIDTH ** -0.5, 0.09375, ((2, 4),))
    adapter_up = scatter_about(part_splits[4], (ADAPTERS, R, FF), (FF // 16) ** -0.5, 0.1875, ((2, 4),))
    tenant_ids = draw_tenant_ids(jax.random.fold_in(jax.random.fold_in(key_list[8], part), 71), part)
    tenant_token_counts = draw_tenant_token_counts(jax.random.fold_in(jax.random.fold_in(key_list[8], part), 71), part)
    owner_map = draw_owner_map(jax.random.fold_in(key_list[8], 71), part)
    return {"tokens": tokens, "grad_out": grad_out, "frozen_weight": frozen_weight, "adapter_down": adapter_down, "adapter_up": adapter_up, "tenant_ids": tenant_ids, "tenant_token_counts": tenant_token_counts, "owner_map": owner_map}


adapter_scale = 2.0


def slot_numbers(owner_map, slot_count):
    positions = jnp.arange(owner_map.shape[0])
    same_owner = owner_map[:, None] == owner_map[None, :]
    earlier = positions[:, None] > positions[None, :]
    owner_rank = jnp.sum((same_owner & earlier).astype(jnp.int32), axis=1).astype(jnp.int32)
    return (owner_map.astype(jnp.int32) * slot_count + owner_rank).astype(jnp.int32)


def reference(tokens, grad_out, frozen_weight, adapter_down, adapter_up, tenant_ids, tenant_token_counts, owner_map):
    shard_ff = FF // N_TENSOR
    shard_d = MODEL_WIDTH // N_TENSOR
    tile_tenant = tenant_ids.reshape(N_DP * TILES, TILE)[:, 0]
    weight_wide = frozen_weight.astype(jnp.float32).reshape(MODEL_WIDTH, N_TENSOR, shard_ff)
    block_of_columns = (jnp.arange(MODEL_WIDTH)[None, :] // shard_d) == jnp.arange(N_TENSOR)[:, None]

    def one_group(inputs):
        rows_x, rows_dy, selected_slot = inputs
        down_tile_list = adapter_down[selected_slot].astype(jnp.float32)
        up_tiles = adapter_up[selected_slot].astype(jnp.float32)
        x_tiles = rows_x.astype(jnp.float32).reshape(TILES, TILE, MODEL_WIDTH)
        dy_tiles = rows_dy.astype(jnp.float32).reshape(TILES, TILE, FF)
        middle = jnp.einsum("krd,ktd->krt", down_tile_list, x_tiles).astype(jnp.bfloat16)
        backward_result = jnp.einsum("krf,ktf->krt", up_tiles, dy_tiles).astype(jnp.bfloat16)
        dy_wide = rows_dy.astype(jnp.float32).reshape(GROUP_TOKENS, N_TENSOR, shard_ff)
        frozen_term = jnp.einsum("tjf,djf->jtd", dy_wide, weight_wide).astype(jnp.bfloat16)
        adapter_input = adapter_scale * jnp.einsum("gqx,gqj->gxj", backward_result.astype(jnp.float32), down_tile_list).reshape(GROUP_TOKENS, MODEL_WIDTH)
        gradient_terms = frozen_term.astype(jnp.float32) + jnp.where(block_of_columns[:, None, :], adapter_input[None], 0.0)
        summed = jnp.sum(gradient_terms.astype(jnp.bfloat16).astype(jnp.float32), axis=0).astype(jnp.bfloat16)
        per_tile_scale = adapter_scale / tenant_token_counts[selected_slot].astype(jnp.float32)
        tile_up = (per_tile_scale[:, None, None] * jnp.einsum("krt,ktf->krf", middle.astype(jnp.float32), dy_tiles)).astype(jnp.bfloat16)
        tile_down = (per_tile_scale[:, None, None] * jnp.einsum("krt,ktd->krd", backward_result.astype(jnp.float32), x_tiles)).astype(jnp.bfloat16)
        return summed, tile_down, tile_up

    grouped = lax.map(one_group, (tokens.reshape(N_DP, GROUP_TOKENS, MODEL_WIDTH), grad_out.reshape(N_DP, GROUP_TOKENS, FF), tile_tenant.reshape(N_DP, TILES)))
    input_grad = grouped[0].reshape(TOKENS, MODEL_WIDTH)
    down_all = grouped[1].reshape(N_DP * TILES, R, MODEL_WIDTH).astype(jnp.float32)
    up_all = grouped[2].reshape(N_DP * TILES, R, FF).astype(jnp.float32)
    dense_down = jax.ops.segment_sum(down_all, tile_tenant, ADAPTERS)
    dense_up = jax.ops.segment_sum(up_all, tile_tenant, ADAPTERS)
    slot_of = slot_numbers(owner_map, SLOTS)
    select = (jnp.arange(OWNED)[:, None] == slot_of[None, :]).astype(jnp.float32)
    grad_down = jnp.einsum("oa,ard->ord", select, dense_down, precision=lax.Precision.HIGHEST)
    grad_up = jnp.einsum("oa,arf->orf", select, dense_up, precision=lax.Precision.HIGHEST)
    return (input_grad, grad_down, grad_up)
```

```python
import jax
import jax.numpy as jnp
from jax import lax
from jax.experimental import pallas as pl
from jax.experimental.pallas import tpu as pltpu
from jax.sharding import PartitionSpec as P

TILE = 128


adapter_scale = 2.0


def owner_slots(owner_map, slot_count):
    positions = jnp.arange(owner_map.shape[0])
    same_owner = owner_map[:, None] == owner_map[None, :]
    earlier = positions[:, None] > positions[None, :]
    owner_rank = jnp.sum((same_owner & earlier).astype(jnp.int32), axis=1)
    return owner_map * slot_count + owner_rank


def dot_last(a, b):
    return lax.dot_general(a, b, (((1,), (1,)), ((), ())), preferred_element_type=jnp.float32)


def place_kernel(slots_ref, tiles_ref, up_ref, down_ref):
    per_step = up_ref.shape[0]
    ff_shard = up_ref.shape[2]
    first = pl.program_id(0) * per_step
    up_ref[...] = jnp.zeros_like(up_ref)
    down_ref[...] = jnp.zeros_like(down_ref)

    def add_tile(k, carry):
        local = slots_ref[k] - first

        @pl.when((local >= 0) & (local < per_step))
        def _():
            up_ref[local] += tiles_ref[k, :, :ff_shard].astype(jnp.float32)
            down_ref[local] += tiles_ref[k, :, ff_shard:].astype(jnp.float32)

        return carry

    lax.fori_loop(0, tiles_ref.shape[0], add_tile, 0)


def place_in_slots(tiles, slots, slot_count, ff_shard):
    tile_count, rank, columns = tiles.shape
    per_step = min(4, slot_count)
    return pl.pallas_call(
        place_kernel,
        grid_spec=pltpu.PrefetchScalarGridSpec(
            num_scalar_prefetch=1,
            grid=(slot_count // per_step,),
            in_specs=[pl.BlockSpec((tile_count, rank, columns), lambda i, s: (0, 0, 0))],
            out_specs=[
                pl.BlockSpec((per_step, rank, ff_shard), lambda i, s: (i, 0, 0)),
                pl.BlockSpec((per_step, rank, columns - ff_shard), lambda i, s: (i, 0, 0)),
            ],
        ),
        out_shape=[
            jax.ShapeDtypeStruct((slot_count, rank, ff_shard), jnp.float32),
            jax.ShapeDtypeStruct((slot_count, rank, columns - ff_shard), jnp.float32),
        ],
        compiler_params=pltpu.CompilerParams(vmem_limit_bytes=32 * 1024 * 1024),
    )(slots, tiles)


def adapter_parts(tokens, grad_out, adapter_down, adapter_up, tenants, counts):
    tile_count = tenants.shape[0]
    shard_index = lax.axis_index("tensor")
    down_sel = adapter_down[tenants]
    up_sel = adapter_up[tenants]
    dy_tiles = grad_out.reshape(tile_count, TILE, -1)
    own_down = lax.all_to_all(down_sel, "tensor", split_axis=0, concat_axis=2, tiled=True)[0]
    middle = dot_last(own_down, tokens).astype(jnp.bfloat16)
    backed_part = jnp.einsum(
        "krf,ktf->krt", up_sel, dy_tiles, preferred_element_type=jnp.float32
    ).astype(jnp.bfloat16)
    sent = jnp.concatenate([backed_part, jnp.broadcast_to(middle, backed_part.shape)], axis=1)
    got = lax.all_to_all(sent, "tensor", split_axis=0, concat_axis=0, tiled=True)
    rank = middle.shape[0]
    backed = jnp.sum(got[:, :rank].astype(jnp.float32), axis=0).astype(jnp.bfloat16)
    middle_all = got[:, rank:]
    scale = adapter_scale / counts[tenants].astype(jnp.float32)
    tile_up = (
        scale[:, None, None]
        * jnp.einsum("krt,ktf->krf", middle_all, dy_tiles, preferred_element_type=jnp.float32)
    ).astype(jnp.bfloat16)
    own_tile_down = (
        scale[shard_index] * jnp.dot(backed, tokens, preferred_element_type=jnp.float32)
    ).astype(jnp.bfloat16)
    tile_down = lax.all_to_all(own_tile_down, "tensor", split_axis=1, concat_axis=0, tiled=True)
    tile_down = tile_down.reshape(tile_count, rank, -1)
    return own_down, backed, jnp.concatenate([tile_up, tile_down], axis=2)


def sum_over_tensor(terms):
    index = lax.axis_index("tensor")
    chip, core = index // 2, index % 2
    rows = terms.shape[-2] // 4
    split = terms.reshape(terms.shape[:-2] + (2, 2, rows, terms.shape[-1]))
    axis = split.ndim - 3
    away = lax.dynamic_index_in_dim(split, 1 - core, axis, keepdims=False)
    home = lax.dynamic_index_in_dim(split, core, axis, keepdims=False)
    got = lax.ppermute(away, "tensor", [(0, 1), (1, 0), (2, 3), (3, 2)])
    pair = (home.astype(jnp.float32) + got.astype(jnp.float32)).astype(jnp.bfloat16)
    axis = pair.ndim - 3
    away = lax.dynamic_index_in_dim(pair, 1 - chip, axis, keepdims=False)
    home = lax.dynamic_index_in_dim(pair, chip, axis, keepdims=False)
    got = lax.ppermute(away, "tensor", [(0, 2), (2, 0), (1, 3), (3, 1)])
    return (home.astype(jnp.float32) + got.astype(jnp.float32)).astype(jnp.bfloat16)


def line_of_four(
    tokens,
    grad_out,
    frozen_weight,
    adapter_down,
    adapter_up,
    tenant_ids,
    tenant_token_counts,
    owner_map,
):
    z = lax.axis_index("dp")
    rep = lax.axis_index("rep")
    rows_group, ff_shard = grad_out.shape
    tile_count = rows_group // TILE
    adapter_count = adapter_down.shape[0]
    slot_count = 2 * adapter_count // 4
    partner = [(0, 1), (1, 0), (2, 3), (3, 2)]
    swap_rep = [(0, 1), (1, 0)]
    all_tenants = tenant_ids.reshape(-1, TILE)[:, 0]
    tenants = lax.dynamic_slice_in_dim(all_tenants, z * tile_count, tile_count)

    half = frozen_weight.shape[0] // 2
    n1, n2 = 2, 4

    def piece(k, n):
        return lax.dynamic_slice_in_dim(frozen_weight, rep * half + k * (half // n), half // n, 0)

    partner_dy = lax.ppermute(grad_out, "dp", partner)
    near = [lax.ppermute(piece(k, n1), "dp", [(1, 2), (2, 1)]) for k in range(n1)]
    far = []
    for k in range(n2):
        sent = piece(k, n2)
        if k < 2:
            sent, _ = lax.optimization_barrier((sent, partner_dy))
        else:
            sent, _ = lax.optimization_barrier((sent, far[k - 2]))
        far.append(lax.ppermute(sent, "dp", [(0, 2), (3, 1)]))

    own_down, backed, tile_grads = adapter_parts(
        tokens, grad_out, adapter_down, adapter_up, tenants, tenant_token_counts
    )

    own_block = sum_over_tensor(dot_last(grad_out, frozen_weight).astype(jnp.bfloat16))
    block_for_partner = sum_over_tensor(dot_last(partner_dy, frozen_weight).astype(jnp.bfloat16))
    partner_block = lax.ppermute(block_for_partner, "dp", partner)

    inner = (z == 1) | (z == 2)

    def across(pieces):
        low, high = [], []
        for mine in pieces:
            other = lax.ppermute(mine, "rep", swap_rep)
            terms = jnp.stack(
                [
                    jnp.concatenate(
                        [dot_last(dy, w).astype(jnp.bfloat16) for w in (mine, other)], axis=1
                    )
                    for dy in (grad_out, partner_dy)
                ]
            )
            summed = sum_over_tensor(terms)
            got = lax.ppermute(summed[1], "dp", [(1, 0), (2, 3)])
            block = jnp.where(inner, summed[0], got)
            n = mine.shape[0]
            low.append(jnp.where(rep == 0, block[:, :n], block[:, n:]))
            high.append(jnp.where(rep == 0, block[:, n:], block[:, :n]))
        return jnp.concatenate(low + high, axis=1)

    near_block = across(near)
    far_block = across(far)

    lora = adapter_scale * lax.dot_general(
        backed, own_down, (((0,), (0,)), ((), ())), preferred_element_type=jnp.float32
    )
    even = z % 2 == 0
    first = jnp.where(even, own_block, partner_block)
    second = jnp.where(even, partner_block, own_block)
    left = z < 2
    frozen = jnp.concatenate(
        [
            jnp.where(left, first, far_block),
            jnp.where(left, second, near_block),
            jnp.where(left, near_block, first),
            jnp.where(left, far_block, second),
        ],
        axis=1,
    )
    input_grad = (frozen.astype(jnp.float32) + lora).astype(jnp.bfloat16)

    all_grads = lax.all_gather(tile_grads, "dp", axis=0, tiled=True)
    slots = owner_slots(owner_map, slot_count)[all_tenants] - z * slot_count
    grad_up, grad_down = place_in_slots(all_grads, slots, slot_count, ff_shard)
    return input_grad, grad_down, grad_up


def any_line(
    tokens,
    grad_out,
    frozen_weight,
    adapter_down,
    adapter_up,
    tenant_ids,
    tenant_token_counts,
    owner_map,
):
    dp_count = lax.axis_size("dp")
    group_index = lax.axis_index("dp")
    shard_index = lax.axis_index("tensor")
    rows_group, ff_shard = grad_out.shape
    width_shard = adapter_down.shape[2]
    adapter_count = adapter_down.shape[0]
    tile_count = rows_group // TILE
    slot_count = 2 * adapter_count // dp_count
    all_tenants = tenant_ids.reshape(-1, TILE)[:, 0]
    tenants = lax.dynamic_slice_in_dim(all_tenants, group_index * tile_count, tile_count)
    columns = lax.all_to_all(tokens, "tensor", split_axis=1, concat_axis=0, tiled=True)
    down_sel = adapter_down[tenants]
    up_sel = adapter_up[tenants]
    x_tiles = columns.reshape(tile_count, TILE, width_shard)
    dy_tiles = grad_out.reshape(tile_count, TILE, ff_shard)
    middle_part = jnp.einsum("krd,ktd->krt", down_sel, x_tiles, preferred_element_type=jnp.float32)
    backed_part = jnp.einsum("krf,ktf->krt", up_sel, dy_tiles, preferred_element_type=jnp.float32)
    middle = lax.psum(middle_part.astype(jnp.bfloat16), "tensor")
    backed = lax.psum(backed_part.astype(jnp.bfloat16), "tensor")
    whole = lax.all_gather(frozen_weight, "dp", axis=0, tiled=True)
    frozen = dot_last(grad_out, whole).astype(jnp.bfloat16).astype(jnp.float32)
    lora = adapter_scale * jnp.einsum(
        "krt,krd->ktd", backed, down_sel, preferred_element_type=jnp.float32
    ).reshape(rows_group, width_shard)
    start = shard_index * width_shard
    block = lax.dynamic_slice_in_dim(frozen, start, width_shard, 1) + lora
    terms = lax.dynamic_update_slice_in_dim(frozen, block, start, 1).astype(jnp.bfloat16)
    input_grad = lax.psum_scatter(terms, "tensor", scatter_dimension=0, tiled=True)
    scale = (adapter_scale / tenant_token_counts[tenants].astype(jnp.float32))[:, None, None]
    tile_up = scale * jnp.einsum(
        "krt,ktf->krf", middle, dy_tiles, preferred_element_type=jnp.float32
    )
    tile_down = scale * jnp.einsum(
        "krt,ktd->krd", backed, x_tiles, preferred_element_type=jnp.float32
    )
    tile_grads = jnp.concatenate([tile_up, tile_down], axis=2).astype(jnp.bfloat16)
    all_grads = lax.all_gather(tile_grads, "dp", axis=0, tiled=True)
    slots = owner_slots(owner_map, slot_count)[all_tenants] - group_index * slot_count
    grad_up, grad_down = place_in_slots(all_grads, slots, slot_count, ff_shard)
    return input_grad, grad_down, grad_up


def solution(mesh):
    sizes = mesh.shape
    four = sizes["dp"] == 4 and sizes["tensor"] == 4 and sizes["rep"] == 2
    placed = (
        P(("rep", "dp", "tensor"), None),
        P(("rep", "dp"), "tensor"),
        P("dp", "tensor"),
        P("rep", None, "tensor"),
        P("rep", None, "tensor"),
        P("rep"),
        P("rep"),
        P(),
    )
    return jax.shard_map(
        line_of_four if four else any_line,
        mesh=mesh,
        in_specs=placed,
        out_specs=(
            P(("rep", "dp", "tensor"), None),
            P(("rep", "dp"), None, "tensor"),
            P(("rep", "dp"), None, "tensor"),
        ),
        check_vma=False,
    )
```

```python
import jax
import jax.numpy as jnp
from jax import lax
from jax.experimental import pallas as pl
from jax.experimental.pallas import tpu as pltpu
from jax.sharding import PartitionSpec as P

TILE = 128


adapter_scale = 2.0


def owner_slots(owner_map, slot_count):
    positions = jnp.arange(owner_map.shape[0])
    same_owner = owner_map[:, None] == owner_map[None, :]
    earlier = positions[:, None] > positions[None, :]
    owner_rank = jnp.sum((same_owner & earlier).astype(jnp.int32), axis=1)
    return owner_map * slot_count + owner_rank


def dot_last(a, b):
    return lax.dot_general(a, b, (((1,), (1,)), ((), ())), preferred_element_type=jnp.float32)


def place_kernel(slots_ref, *refs):
    *tile_refs, up_ref, down_ref = refs
    per_step = up_ref.shape[0]
    ff_shard = up_ref.shape[2]
    tiles_each = tile_refs[0].shape[0]
    first = pl.program_id(0) * per_step
    up_ref[...] = jnp.zeros_like(up_ref)
    down_ref[...] = jnp.zeros_like(down_ref)
    for i, tiles_ref in enumerate(tile_refs):
        for k in range(tiles_each):
            local = slots_ref[i * tiles_each + k] - first

            @pl.when((local >= 0) & (local < per_step))
            def _(tiles_ref=tiles_ref, k=k, local=local):
                up_ref[local] += tiles_ref[k, :, :ff_shard].astype(jnp.float32)
                down_ref[local] += tiles_ref[k, :, ff_shard:].astype(jnp.float32)


def place_in_slots(groups, slots, slot_count, ff_shard):
    tile_count, rank, columns = groups[0].shape
    per_step = min(4, slot_count)
    return pl.pallas_call(
        place_kernel,
        grid_spec=pltpu.PrefetchScalarGridSpec(
            num_scalar_prefetch=1,
            grid=(slot_count // per_step,),
            in_specs=[pl.BlockSpec((tile_count, rank, columns), lambda i, s: (0, 0, 0))]
            * len(groups),
            out_specs=[
                pl.BlockSpec((per_step, rank, ff_shard), lambda i, s: (i, 0, 0)),
                pl.BlockSpec((per_step, rank, columns - ff_shard), lambda i, s: (i, 0, 0)),
            ],
        ),
        out_shape=[
            jax.ShapeDtypeStruct((slot_count, rank, ff_shard), jnp.float32),
            jax.ShapeDtypeStruct((slot_count, rank, columns - ff_shard), jnp.float32),
        ],
        compiler_params=pltpu.CompilerParams(vmem_limit_bytes=32 * 1024 * 1024),
    )(slots, *groups)


def terms_kernel(place_ref, own_ref, partner_ref, *refs):
    *weight_refs, away_ref, home_ref = refs
    chip = place_ref[0]
    depth = own_ref.shape[-1]

    def products(dy_ref, out_ref):
        dy = dy_ref[...].reshape(2 * TILE, depth)
        column = 0
        for weight_ref in weight_refs:
            rows = weight_ref.shape[0]
            step = min(rows, 512)
            for start in range(0, rows, step):
                part = dot_last(dy, weight_ref[start : start + step]).astype(jnp.bfloat16)
                out_ref[1 - chip, 0, :, column : column + step] = part[:TILE]
                out_ref[chip, 0, :, column : column + step] = part[TILE:]
                column += step

    for side, out_ref in ((0, away_ref), (1, home_ref)):
        for group, dy_ref in ((0, own_ref), (1, partner_ref)):

            @pl.when((pl.program_id(0) == side) & (pl.program_id(1) == group))
            def _(dy_ref=dy_ref, out_ref=out_ref):
                products(dy_ref, out_ref)


def product_terms(dy, partner_dy, weights, place):
    depth = dy.shape[1]
    columns = sum(w.shape[0] for w in weights)
    split = (2, 2, TILE, depth)
    out = jax.ShapeDtypeStruct((2, 2, TILE, columns), jnp.bfloat16)

    def rows_of(side, group, place):
        return (0, jnp.where(side == 0, 1 - place[1], place[1]), 0, 0)

    dy_spec = pl.BlockSpec((2, 1, TILE, depth), rows_of)
    return pl.pallas_call(
        terms_kernel,
        grid_spec=pltpu.PrefetchScalarGridSpec(
            num_scalar_prefetch=1,
            grid=(2, 2),
            in_specs=[dy_spec, dy_spec]
            + [
                pl.BlockSpec(w.shape, lambda s, g, p: (0, 0), pipeline_mode=pl.Buffered(1))
                for w in weights
            ],
            out_specs=[
                pl.BlockSpec(
                    (2, 1, TILE, columns), lambda s, g, p: (0, jnp.where(s == 0, g, 1), 0, 0)
                ),
                pl.BlockSpec(
                    (2, 1, TILE, columns), lambda s, g, p: (0, jnp.where(s == 0, 0, g), 0, 0)
                ),
            ],
        ),
        out_shape=[out, out],
        compiler_params=pltpu.CompilerParams(vmem_limit_bytes=48 * 1024 * 1024),
        cost_estimate=pl.CostEstimate(flops=1000, bytes_accessed=1000, transcendentals=0),
    )(place, dy.reshape(split), partner_dy.reshape(split), *weights)


def adapter_parts(tokens, grad_out, adapter_down, adapter_up, tenants, counts):
    tile_count = tenants.shape[0]
    shard_index = lax.axis_index("tensor")
    down_sel = adapter_down[tenants]
    up_sel = adapter_up[tenants]
    dy_tiles = grad_out.reshape(tile_count, TILE, -1)
    own_down = lax.all_to_all(down_sel, "tensor", split_axis=0, concat_axis=2, tiled=True)[0]
    middle = dot_last(own_down, tokens).astype(jnp.bfloat16)
    backed_part = jnp.einsum(
        "krf,ktf->krt", up_sel, dy_tiles, preferred_element_type=jnp.float32
    ).astype(jnp.bfloat16)
    sent = jnp.concatenate([backed_part, jnp.broadcast_to(middle, backed_part.shape)], axis=1)
    got = lax.all_to_all(sent, "tensor", split_axis=0, concat_axis=0, tiled=True)
    rank = middle.shape[0]
    backed = jnp.sum(got[:, :rank].astype(jnp.float32), axis=0).astype(jnp.bfloat16)
    middle_all = got[:, rank:]
    scale = adapter_scale / counts[tenants].astype(jnp.float32)
    tile_up = (
        scale[:, None, None]
        * jnp.einsum("krt,ktf->krf", middle_all, dy_tiles, preferred_element_type=jnp.float32)
    ).astype(jnp.bfloat16)
    own_tile_down = (
        scale[shard_index] * jnp.dot(backed, tokens, preferred_element_type=jnp.float32)
    ).astype(jnp.bfloat16)
    tile_down = lax.all_to_all(own_tile_down, "tensor", split_axis=1, concat_axis=0, tiled=True)
    tile_down = tile_down.reshape(tile_count, rank, -1)
    return own_down, backed, jnp.concatenate([tile_up, tile_down], axis=2)


def sum_over_tensor(away, home):
    got = lax.ppermute(away, "tensor", [(0, 1), (1, 0), (2, 3), (3, 2)])
    pair = home.astype(jnp.float32) + got.astype(jnp.float32)
    got = lax.ppermute(pair[0].astype(jnp.bfloat16), "tensor", [(0, 2), (2, 0), (1, 3), (3, 1)])
    return pair[1] + got.astype(jnp.float32)


PARTNER = [(0, 1), (1, 0), (2, 3), (3, 2)]
MIDDLE = [(1, 2), (2, 1)]
OUTER_TO_MIDDLE = [(0, 2), (3, 1)]
OUTWARD = [(1, 0), (2, 3)]


def line_of_four(
    tokens,
    grad_out,
    frozen_weight,
    adapter_down,
    adapter_up,
    tenant_ids,
    tenant_token_counts,
    owner_map,
):
    z = lax.axis_index("dp")
    rep = lax.axis_index("rep")
    shard = lax.axis_index("tensor")
    place = jnp.stack([shard // 2, shard % 2]).astype(jnp.int32)
    rows_group, ff_shard = grad_out.shape
    tile_count = rows_group // TILE
    adapter_count = adapter_down.shape[0]
    slot_count = 2 * adapter_count // 4
    inner = (z == 1) | (z == 2)
    all_tenants = tenant_ids.reshape(-1, TILE)[:, 0]
    tenants = lax.dynamic_slice_in_dim(all_tenants, z * tile_count, tile_count)

    width = frozen_weight.shape[0]
    half = width // 2
    pieces = 4
    rows = half // pieces

    def piece(k):
        return lax.dynamic_slice_in_dim(frozen_weight, rep * half + k * rows, rows, 0)

    def swap_rep(w):
        return lax.ppermute(w, "rep", [(0, 1), (1, 0)])

    partner_dy = lax.ppermute(grad_out, "dp", PARTNER)
    near = [lax.ppermute(piece(k), "dp", MIDDLE) for k in range(pieces)]
    far = [lax.ppermute(piece(k), "dp", OUTER_TO_MIDDLE) for k in range(pieces)]
    near_pairs = [(w, swap_rep(w)) for w in near]
    far_pairs = [(w, swap_rep(w)) for w in far]

    own_down, backed, tile_grads = adapter_parts(
        tokens, grad_out, adapter_down, adapter_up, tenants, tenant_token_counts
    )
    partner_grads = lax.ppermute(tile_grads, "dp", PARTNER)
    near_grads = lax.ppermute(tile_grads, "dp", MIDDLE)
    far_grads = lax.ppermute(partner_grads, "dp", MIDDLE)
    near_grads_out = lax.ppermute(near_grads, "dp", OUTWARD)
    far_grads_out = lax.ppermute(far_grads, "dp", OUTWARD)

    first_weights = [frozen_weight] + [w for pair in near_pairs for w in pair]
    summed = sum_over_tensor(*product_terms(grad_out, partner_dy, first_weights, place))
    own_first = summed[0].astype(jnp.bfloat16)
    got_first = lax.ppermute(summed[1].astype(jnp.bfloat16), "dp", PARTNER)
    own_block, partner_block = own_first[:, :width], got_first[:, :width]

    def in_order(columns):
        pairs = columns.reshape(TILE, -1, 2, rows)
        mine = pairs[:, :, 0].reshape(TILE, half)
        other = pairs[:, :, 1].reshape(TILE, half)
        return jnp.concatenate(
            [jnp.where(rep == 0, mine, other), jnp.where(rep == 0, other, mine)], axis=1
        )

    near_block = in_order(jnp.where(inner, own_first[:, width:], got_first[:, width:]))
    far_columns = []
    for pair in far_pairs:
        summed = sum_over_tensor(*product_terms(grad_out, partner_dy, pair, place))
        got = lax.ppermute(summed[1].astype(jnp.bfloat16), "dp", OUTWARD)
        far_columns.append(jnp.where(inner, summed[0].astype(jnp.bfloat16), got))
    far_block = in_order(jnp.concatenate(far_columns, axis=1))

    lora = adapter_scale * lax.dot_general(
        backed, own_down, (((0,), (0,)), ((), ())), preferred_element_type=jnp.float32
    )
    even = z % 2 == 0
    first = jnp.where(even, own_block, partner_block)
    second = jnp.where(even, partner_block, own_block)
    left = z < 2
    frozen = jnp.concatenate(
        [
            jnp.where(left, first, far_block),
            jnp.where(left, second, near_block),
            jnp.where(left, near_block, first),
            jnp.where(left, far_block, second),
        ],
        axis=1,
    )
    input_grad = (frozen.astype(jnp.float32) + lora).astype(jnp.bfloat16)

    partner_index = z + 1 - 2 * (z % 2)
    near_index = jnp.where(z < 2, 2, 1)
    far_index = jnp.where(z < 2, 3, 0)
    tile_slots = owner_slots(owner_map, slot_count)[all_tenants].reshape(4, tile_count)
    tile_slots = tile_slots - z * slot_count
    nowhere = jnp.full((tile_count,), -1, jnp.int32)
    slots = jnp.concatenate(
        [
            tile_slots[z],
            tile_slots[partner_index],
            jnp.where(inner, tile_slots[near_index], nowhere),
            jnp.where(inner, tile_slots[far_index], nowhere),
            jnp.where(inner, nowhere, tile_slots[near_index]),
            jnp.where(inner, nowhere, tile_slots[far_index]),
        ]
    )
    grad_up, grad_down = place_in_slots(
        [tile_grads, partner_grads, near_grads, far_grads, near_grads_out, far_grads_out],
        slots,
        slot_count,
        ff_shard,
    )
    return input_grad, grad_down, grad_up


def any_line(
    tokens,
    grad_out,
    frozen_weight,
    adapter_down,
    adapter_up,
    tenant_ids,
    tenant_token_counts,
    owner_map,
):
    dp_count = lax.axis_size("dp")
    group_index = lax.axis_index("dp")
    shard_index = lax.axis_index("tensor")
    rows_group, ff_shard = grad_out.shape
    width_shard = adapter_down.shape[2]
    adapter_count = adapter_down.shape[0]
    tile_count = rows_group // TILE
    slot_count = 2 * adapter_count // dp_count
    all_tenants = tenant_ids.reshape(-1, TILE)[:, 0]
    tenants = lax.dynamic_slice_in_dim(all_tenants, group_index * tile_count, tile_count)
    columns = lax.all_to_all(tokens, "tensor", split_axis=1, concat_axis=0, tiled=True)
    down_sel = adapter_down[tenants]
    up_sel = adapter_up[tenants]
    x_tiles = columns.reshape(tile_count, TILE, width_shard)
    dy_tiles = grad_out.reshape(tile_count, TILE, ff_shard)
    middle_part = jnp.einsum("krd,ktd->krt", down_sel, x_tiles, preferred_element_type=jnp.float32)
    backed_part = jnp.einsum("krf,ktf->krt", up_sel, dy_tiles, preferred_element_type=jnp.float32)
    middle = lax.psum(middle_part.astype(jnp.bfloat16), "tensor")
    backed = lax.psum(backed_part.astype(jnp.bfloat16), "tensor")
    whole = lax.all_gather(frozen_weight, "dp", axis=0, tiled=True)
    frozen = dot_last(grad_out, whole).astype(jnp.bfloat16).astype(jnp.float32)
    lora = adapter_scale * jnp.einsum(
        "krt,krd->ktd", backed, down_sel, preferred_element_type=jnp.float32
    ).reshape(rows_group, width_shard)
    start = shard_index * width_shard
    block = lax.dynamic_slice_in_dim(frozen, start, width_shard, 1) + lora
    terms = lax.dynamic_update_slice_in_dim(frozen, block, start, 1).astype(jnp.bfloat16)
    input_grad = lax.psum_scatter(terms, "tensor", scatter_dimension=0, tiled=True)
    scale = (adapter_scale / tenant_token_counts[tenants].astype(jnp.float32))[:, None, None]
    tile_up = scale * jnp.einsum(
        "krt,ktf->krf", middle, dy_tiles, preferred_element_type=jnp.float32
    )
    tile_down = scale * jnp.einsum(
        "krt,ktd->krd", backed, x_tiles, preferred_element_type=jnp.float32
    )
    tile_grads = jnp.concatenate([tile_up, tile_down], axis=2).astype(jnp.bfloat16)
    all_grads = lax.all_gather(tile_grads, "dp", axis=0, tiled=True)
    slots = owner_slots(owner_map, slot_count)[all_tenants] - group_index * slot_count
    grad_up, grad_down = place_in_slots([all_grads], slots, slot_count, ff_shard)
    return input_grad, grad_down, grad_up


def solution(mesh):
    sizes = mesh.shape
    four = sizes["dp"] == 4 and sizes["tensor"] == 4 and sizes["rep"] == 2
    placed = (
        P(("rep", "dp", "tensor"), None),
        P(("rep", "dp"), "tensor"),
        P("dp", "tensor"),
        P("rep", None, "tensor"),
        P("rep", None, "tensor"),
        P("rep"),
        P("rep"),
        P(),
    )
    return jax.shard_map(
        line_of_four if four else any_line,
        mesh=mesh,
        in_specs=placed,
        out_specs=(
            P(("rep", "dp", "tensor"), None),
            P(("rep", "dp"), None, "tensor"),
            P(("rep", "dp"), None, "tensor"),
        ),
        check_vma=False,
    )
```

```python
import functools

import jax
import jax.numpy as jnp
from jax import lax
from jax.experimental import pallas as pl
from jax.experimental.pallas import tpu as pltpu
from jax.sharding import PartitionSpec as P

TILE = 128


adapter_scale = 2.0


def owner_slots(owner_map, slot_count):
    positions = jnp.arange(owner_map.shape[0])
    same_owner = owner_map[:, None] == owner_map[None, :]
    earlier = positions[:, None] > positions[None, :]
    owner_rank = jnp.sum((same_owner & earlier).astype(jnp.int32), axis=1)
    return owner_map * slot_count + owner_rank


def dot_last(a, b):
    return lax.dot_general(a, b, (((1,), (1,)), ((), ())), preferred_element_type=jnp.float32)


def place_kernel(slots_ref, *refs):
    *tile_refs, up_ref, down_ref = refs
    per_step = up_ref.shape[0]
    ff_shard = up_ref.shape[2]
    tiles_each = tile_refs[0].shape[0]
    first = pl.program_id(0) * per_step
    up_ref[...] = jnp.zeros_like(up_ref)
    down_ref[...] = jnp.zeros_like(down_ref)
    for i, tiles_ref in enumerate(tile_refs):
        for k in range(tiles_each):
            local = slots_ref[i * tiles_each + k] - first

            @pl.when((local >= 0) & (local < per_step))
            def _(tiles_ref=tiles_ref, k=k, local=local):
                up_ref[local] += tiles_ref[k, :, :ff_shard].astype(jnp.float32)
                down_ref[local] += tiles_ref[k, :, ff_shard:].astype(jnp.float32)


def place_in_slots(groups, slots, slot_count, ff_shard):
    tile_count, rank, columns = groups[0].shape
    per_step = min(4, slot_count)
    return pl.pallas_call(
        place_kernel,
        grid_spec=pltpu.PrefetchScalarGridSpec(
            num_scalar_prefetch=1,
            grid=(slot_count // per_step,),
            in_specs=[pl.BlockSpec((tile_count, rank, columns), lambda i, s: (0, 0, 0))]
            * len(groups),
            out_specs=[
                pl.BlockSpec((per_step, rank, ff_shard), lambda i, s: (i, 0, 0)),
                pl.BlockSpec((per_step, rank, columns - ff_shard), lambda i, s: (i, 0, 0)),
            ],
        ),
        out_shape=[
            jax.ShapeDtypeStruct((slot_count, rank, ff_shard), jnp.float32),
            jax.ShapeDtypeStruct((slot_count, rank, columns - ff_shard), jnp.float32),
        ],
        compiler_params=pltpu.CompilerParams(vmem_limit_bytes=32 * 1024 * 1024),
    )(slots, *groups)


def terms_kernel(group_count, out_count, place_ref, *refs):
    dy_refs, refs = refs[:group_count], refs[group_count:]
    *refs, dy_buffer, weight_buffer, dy_sems, weight_sems = refs
    weight_refs, out_refs = refs[:-out_count], refs[-out_count:]
    tiles_each = 4 // out_count
    chip, core = place_ref[0], place_ref[1]
    depth = dy_buffer.shape[-1]
    starts = [0]
    for ref in weight_refs:
        starts.append(starts[-1] + ref.shape[0])

    if out_count == 1:
        owners = [(0, 0), (0, 1), (1, 0), (1, 1)]
    else:
        owners = [(1 - chip, 1 - core), (chip, 1 - core), (1 - chip, core), (chip, core)]

    def start_dy(group, slot):
        for k, dy_ref in enumerate(dy_refs):

            @pl.when(group == k)
            def _(dy_ref=dy_ref):
                for i, (x, c) in enumerate(owners):
                    pltpu.make_async_copy(
                        dy_ref.at[x, c],
                        dy_buffer.at[slot, pl.ds(i * TILE, TILE)],
                        dy_sems.at[slot],
                    ).start()

    def wait_dy(slot):
        whole = dy_buffer.at[slot]
        pltpu.make_async_copy(whole, whole, dy_sems.at[slot]).wait()

    start_dy(0, 0)
    for i, (ref, start) in enumerate(zip(weight_refs, starts)):
        for row in range(0, ref.shape[0], 256):
            rows = min(256, ref.shape[0] - row)
            pltpu.make_async_copy(
                ref.at[pl.ds(row, rows)],
                weight_buffer.at[pl.ds(start + row, rows)],
                weight_sems.at[i],
            ).start()

    def one_group(group, carry):
        slot = lax.rem(group, 2)

        @pl.when(group + 1 < group_count)
        def _():
            start_dy(group + 1, 1 - slot)

        wait_dy(slot)
        dy = dy_buffer[slot]

        @pl.when(group == 0)
        def _():
            for i, (start, end) in enumerate(zip(starts[:-1], starts[1:])):
                whole = weight_buffer.at[pl.ds(start, end - start)]
                pltpu.make_async_copy(whole, whole, weight_sems.at[i]).wait()

        for column in range(0, starts[-1], 256):
            stop = min(column + 256, starts[-1])
            part = dot_last(dy, weight_buffer[column:stop]).astype(jnp.bfloat16)
            for k in range(4):
                out_ref = out_refs[k // tiles_each]
                rows = part[k * TILE : (k + 1) * TILE]
                out_ref[k % tiles_each, group, :, column:stop] = rows
        return carry

    lax.fori_loop(0, group_count, one_group, 0)


def product_terms(groups, weights, place, out_count):
    depth = groups[0].shape[1]
    columns = sum(w.shape[0] for w in weights)
    out = jax.ShapeDtypeStruct((4 // out_count, len(groups), TILE, columns), jnp.bfloat16)
    in_hbm = pl.BlockSpec(memory_space=pl.ANY)
    return pl.pallas_call(
        functools.partial(terms_kernel, len(groups), out_count),
        grid_spec=pltpu.PrefetchScalarGridSpec(
            num_scalar_prefetch=1,
            grid=(1,),
            in_specs=[in_hbm] * (len(groups) + len(weights)),
            out_specs=[pl.BlockSpec(out.shape, lambda i, p: (0, 0, 0, 0))] * out_count,
            scratch_shapes=[
                pltpu.VMEM((2, 4 * TILE, depth), jnp.bfloat16),
                pltpu.VMEM((columns, depth), jnp.bfloat16),
                pltpu.SemaphoreType.DMA((2,)),
                pltpu.SemaphoreType.DMA((len(weights),)),
            ],
        ),
        out_shape=[out] * out_count,
        compiler_params=pltpu.CompilerParams(vmem_limit_bytes=60 * 1024 * 1024),
        cost_estimate=pl.CostEstimate(flops=0, bytes_accessed=0, transcendentals=0),
    )(place, *[dy.reshape(2, 2, TILE, depth) for dy in groups], *weights)


def sum_over_tensor(terms):
    away, home = terms
    got = lax.ppermute(away, "tensor", [(0, 1), (1, 0), (2, 3), (3, 2)])
    pair = home.astype(jnp.float32) + got.astype(jnp.float32)
    got = lax.ppermute(pair[0].astype(jnp.bfloat16), "tensor", [(0, 2), (2, 0), (1, 3), (3, 1)])
    return (pair[1] + got.astype(jnp.float32)).astype(jnp.bfloat16)


def sum_by_swap(terms):
    got = lax.all_to_all(terms[0], "tensor", split_axis=0, concat_axis=0, tiled=True)
    return jnp.sum(got.astype(jnp.float32), axis=0).astype(jnp.bfloat16)


PARTNER = [(0, 1), (1, 0), (2, 3), (3, 2)]
MIDDLE = [(1, 2), (2, 1)]
OUTER_TO_MIDDLE = [(0, 2), (3, 1)]
OUTWARD = [(1, 0), (2, 3)]
OTHER_REP = [(0, 1), (1, 0)]
OUTWARD_OTHER_REP = [(4 * r + a, 4 * (1 - r) + b) for r in (0, 1) for a, b in OUTWARD]


def line_of_four(
    tokens,
    grad_out,
    frozen_weight,
    adapter_down,
    adapter_up,
    tenant_ids,
    tenant_token_counts,
    owner_map,
):
    z = lax.axis_index("dp")
    rep = lax.axis_index("rep")
    shard = lax.axis_index("tensor")
    place = jnp.stack([shard // 2, shard % 2]).astype(jnp.int32)
    rows_group, ff_shard = grad_out.shape
    tile_count = rows_group // TILE
    adapter_count, rank = adapter_down.shape[:2]
    slot_count = 2 * adapter_count // 4
    inner = (z == 1) | (z == 2)
    all_tenants = tenant_ids.reshape(-1, TILE)[:, 0]
    tenants = lax.dynamic_slice_in_dim(all_tenants, z * tile_count, tile_count)
    half = frozen_weight.shape[0] // 2

    def after(value, *events):
        return lax.optimization_barrier((value,) + events)[0]

    crossing = lax.dynamic_slice_in_dim(frozen_weight, rep * half, half, 0)
    near = lax.ppermute(crossing, "dp", MIDDLE)
    partner_dy = lax.ppermute(after(grad_out, crossing), "dp", PARTNER)
    other_dy = lax.ppermute(grad_out, "rep", OTHER_REP)

    dy_tiles = grad_out.reshape(tile_count, TILE, ff_shard)
    down_sel = adapter_down[tenants]
    up_sel = adapter_up[tenants]
    own_down = lax.all_to_all(down_sel, "tensor", split_axis=0, concat_axis=2, tiled=True)[0]
    middle = dot_last(own_down, tokens).astype(jnp.bfloat16)
    backed_part = jnp.einsum(
        "krf,ktf->krt", up_sel, dy_tiles, preferred_element_type=jnp.float32
    ).astype(jnp.bfloat16)
    sent = jnp.concatenate([backed_part, jnp.broadcast_to(middle, backed_part.shape)], axis=1)
    got = lax.all_to_all(sent, "tensor", split_axis=0, concat_axis=0, tiled=True)
    backed = jnp.sum(got[:, :rank].astype(jnp.float32), axis=0).astype(jnp.bfloat16)
    middle = got[:, rank:]

    def scale_of(tenants):
        return adapter_scale / tenant_token_counts[tenants].astype(jnp.float32)

    def up_gradients(scale, middle, dy):
        dy = dy.reshape(tile_count, TILE, ff_shard)
        product = jnp.einsum("krt,ktf->krf", middle, dy, preferred_element_type=jnp.float32)
        return (scale[:, None, None] * product).astype(jnp.bfloat16)

    scale = scale_of(tenants)
    tile_up = up_gradients(scale, middle, grad_out)
    own_tile_down = (
        scale[shard] * jnp.dot(backed, tokens, preferred_element_type=jnp.float32)
    ).astype(jnp.bfloat16)
    tile_down = lax.all_to_all(
        own_tile_down, "tensor", split_axis=1, concat_axis=0, tiled=True
    ).reshape(tile_count, rank, -1)
    tile_grads = jnp.concatenate([tile_up, tile_down], axis=2)
    to_partner = jnp.concatenate([middle, tile_down], axis=2)

    from_partner = lax.ppermute(to_partner, "dp", PARTNER)

    partner_index = z + 1 - 2 * (z % 2)
    partner_tenants = lax.dynamic_slice_in_dim(
        all_tenants, partner_index * tile_count, tile_count
    )
    partner_up = up_gradients(
        scale_of(partner_tenants), from_partner[:, :, :TILE], partner_dy
    )
    partner_grads = jnp.concatenate([partner_up, from_partner[:, :, TILE:]], axis=2)
    far = lax.ppermute(after(crossing, partner_grads), "dp", OUTER_TO_MIDDLE)
    partner_other_dy = lax.ppermute(after(partner_dy, other_dy), "rep", OTHER_REP)

    events = (partner_dy, tile_grads, partner_grads)
    own_terms = product_terms([after(grad_out, *events), partner_dy], [frozen_weight], place, 1)
    own_sum = sum_by_swap(own_terms)

    groups = [after(grad_out, near, own_terms[0]), partner_dy, other_dy]
    near_terms = product_terms(groups, [near], place, 1)
    near_sum = sum_by_swap(near_terms)

    near_grads = lax.ppermute(after(tile_grads, own_sum, near_sum), "dp", MIDDLE)
    far_grads = lax.ppermute(after(partner_grads, own_sum, near_sum), "dp", MIDDLE)

    groups = [after(grad_out, own_sum, near_sum), partner_dy, other_dy]
    far_terms = product_terms(groups, [far], place, 2)
    far_sum = sum_over_tensor(far_terms)
    outer_terms = product_terms(
        [after(partner_other_dy, far_terms[0], near_grads)], [near, far], place, 2
    )
    outer_sum = sum_over_tensor(outer_terms)[0]
    partner_block = lax.ppermute(own_sum[1], "dp", PARTNER)
    both_sum = jnp.concatenate([near_sum, far_sum], axis=2)
    both_out = lax.ppermute(both_sum[1], "dp", OUTWARD)
    both_other = lax.ppermute(both_sum[2], "rep", OTHER_REP)
    outer_other = lax.ppermute(outer_sum, ("rep", "dp"), OUTWARD_OTHER_REP)
    near_grads_out = lax.ppermute(near_grads, "dp", OUTWARD)
    far_grads_out = lax.ppermute(far_grads, "dp", OUTWARD)

    mine = jnp.where(inner, both_sum[0], both_out)
    other = jnp.where(inner, both_other, outer_other)
    low = jnp.where(rep == 0, mine, other)
    high = jnp.where(rep == 0, other, mine)
    near_block = jnp.concatenate([low[:, :half], high[:, :half]], axis=1)
    far_block = jnp.concatenate([low[:, half:], high[:, half:]], axis=1)
    own_block = own_sum[0]

    lora = adapter_scale * lax.dot_general(
        backed, own_down, (((0,), (0,)), ((), ())), preferred_element_type=jnp.float32
    )
    even = z % 2 == 0
    first = jnp.where(even, own_block, partner_block)
    second = jnp.where(even, partner_block, own_block)
    left = z < 2
    frozen = jnp.concatenate(
        [
            jnp.where(left, first, far_block),
            jnp.where(left, second, near_block),
            jnp.where(left, near_block, first),
            jnp.where(left, far_block, second),
        ],
        axis=1,
    )
    input_grad = (frozen.astype(jnp.float32) + lora).astype(jnp.bfloat16)

    near_index = jnp.where(z < 2, 2, 1)
    far_index = jnp.where(z < 2, 3, 0)
    tile_slots = owner_slots(owner_map, slot_count)[all_tenants].reshape(4, tile_count)
    tile_slots = tile_slots - z * slot_count
    nowhere = jnp.full((tile_count,), -1, jnp.int32)
    slots = jnp.concatenate(
        [
            tile_slots[z],
            tile_slots[partner_index],
            jnp.where(inner, tile_slots[near_index], nowhere),
            jnp.where(inner, tile_slots[far_index], nowhere),
            jnp.where(inner, nowhere, tile_slots[near_index]),
            jnp.where(inner, nowhere, tile_slots[far_index]),
        ]
    )
    grad_up, grad_down = place_in_slots(
        [tile_grads, partner_grads, near_grads, far_grads, near_grads_out, far_grads_out],
        slots,
        slot_count,
        ff_shard,
    )
    return input_grad, grad_down, grad_up


def any_line(
    tokens,
    grad_out,
    frozen_weight,
    adapter_down,
    adapter_up,
    tenant_ids,
    tenant_token_counts,
    owner_map,
):
    dp_count = lax.axis_size("dp")
    group_index = lax.axis_index("dp")
    shard_index = lax.axis_index("tensor")
    rows_group, ff_shard = grad_out.shape
    width_shard = adapter_down.shape[2]
    adapter_count = adapter_down.shape[0]
    tile_count = rows_group // TILE
    slot_count = 2 * adapter_count // dp_count
    all_tenants = tenant_ids.reshape(-1, TILE)[:, 0]
    tenants = lax.dynamic_slice_in_dim(all_tenants, group_index * tile_count, tile_count)
    columns = lax.all_to_all(tokens, "tensor", split_axis=1, concat_axis=0, tiled=True)
    down_sel = adapter_down[tenants]
    up_sel = adapter_up[tenants]
    x_tiles = columns.reshape(tile_count, TILE, width_shard)
    dy_tiles = grad_out.reshape(tile_count, TILE, ff_shard)
    middle_part = jnp.einsum("krd,ktd->krt", down_sel, x_tiles, preferred_element_type=jnp.float32)
    backed_part = jnp.einsum("krf,ktf->krt", up_sel, dy_tiles, preferred_element_type=jnp.float32)
    middle = lax.psum(middle_part.astype(jnp.bfloat16), "tensor")
    backed = lax.psum(backed_part.astype(jnp.bfloat16), "tensor")
    whole = lax.all_gather(frozen_weight, "dp", axis=0, tiled=True)
    frozen = dot_last(grad_out, whole).astype(jnp.bfloat16).astype(jnp.float32)
    lora = adapter_scale * jnp.einsum(
        "krt,krd->ktd", backed, down_sel, preferred_element_type=jnp.float32
    ).reshape(rows_group, width_shard)
    start = shard_index * width_shard
    block = lax.dynamic_slice_in_dim(frozen, start, width_shard, 1) + lora
    terms = lax.dynamic_update_slice_in_dim(frozen, block, start, 1).astype(jnp.bfloat16)
    input_grad = lax.psum_scatter(terms, "tensor", scatter_dimension=0, tiled=True)
    scale = (adapter_scale / tenant_token_counts[tenants].astype(jnp.float32))[:, None, None]
    tile_up = scale * jnp.einsum(
        "krt,ktf->krf", middle, dy_tiles, preferred_element_type=jnp.float32
    )
    tile_down = scale * jnp.einsum(
        "krt,ktd->krd", backed, x_tiles, preferred_element_type=jnp.float32
    )
    tile_grads = jnp.concatenate([tile_up, tile_down], axis=2).astype(jnp.bfloat16)
    all_grads = lax.all_gather(tile_grads, "dp", axis=0, tiled=True)
    slots = owner_slots(owner_map, slot_count)[all_tenants] - group_index * slot_count
    grad_up, grad_down = place_in_slots([all_grads], slots, slot_count, ff_shard)
    return input_grad, grad_down, grad_up


def solution(mesh):
    sizes = mesh.shape
    four = sizes["dp"] == 4 and sizes["tensor"] == 4 and sizes["rep"] == 2
    placed = (
        P(("rep", "dp", "tensor"), None),
        P(("rep", "dp"), "tensor"),
        P("dp", "tensor"),
        P("rep", None, "tensor"),
        P("rep", None, "tensor"),
        P("rep"),
        P("rep"),
        P(),
    )
    return jax.shard_map(
        line_of_four if four else any_line,
        mesh=mesh,
        in_specs=placed,
        out_specs=(
            P(("rep", "dp", "tensor"), None),
            P(("rep", "dp"), None, "tensor"),
            P(("rep", "dp"), None, "tensor"),
        ),
        check_vma=False,
    )
```

```python
import functools

import jax
import jax.numpy as jnp
from jax import lax
from jax.experimental import pallas as pl
from jax.experimental.pallas import tpu as pltpu
from jax.sharding import PartitionSpec as P

TILE = 128


adapter_scale = 2.0


def owner_slots(owner_map, slot_count):
    positions = jnp.arange(owner_map.shape[0])
    same_owner = owner_map[:, None] == owner_map[None, :]
    earlier = positions[:, None] > positions[None, :]
    owner_rank = jnp.sum((same_owner & earlier).astype(jnp.int32), axis=1)
    return owner_map * slot_count + owner_rank


def dot_last(a, b):
    return lax.dot_general(a, b, (((1,), (1,)), ((), ())), preferred_element_type=jnp.float32)


def place_kernel(slots_ref, *refs):
    *tile_refs, up_ref, down_ref = refs
    per_step = up_ref.shape[0]
    ff_shard = up_ref.shape[2]
    tiles_each = tile_refs[0].shape[0]
    first = pl.program_id(0) * per_step
    up_ref[...] = jnp.zeros_like(up_ref)
    down_ref[...] = jnp.zeros_like(down_ref)
    for i, tiles_ref in enumerate(tile_refs):
        for k in range(tiles_each):
            local = slots_ref[i * tiles_each + k] - first

            @pl.when((local >= 0) & (local < per_step))
            def _(tiles_ref=tiles_ref, k=k, local=local):
                up_ref[local] += tiles_ref[k, :, :ff_shard].astype(jnp.float32)
                down_ref[local] += tiles_ref[k, :, ff_shard:].astype(jnp.float32)


def place_in_slots(groups, slots, slot_count, ff_shard):
    tile_count, rank, columns = groups[0].shape
    per_step = min(4, slot_count)
    return pl.pallas_call(
        place_kernel,
        grid_spec=pltpu.PrefetchScalarGridSpec(
            num_scalar_prefetch=1,
            grid=(slot_count // per_step,),
            in_specs=[pl.BlockSpec((tile_count, rank, columns), lambda i, s: (0, 0, 0))]
            * len(groups),
            out_specs=[
                pl.BlockSpec((per_step, rank, ff_shard), lambda i, s: (i, 0, 0)),
                pl.BlockSpec((per_step, rank, columns - ff_shard), lambda i, s: (i, 0, 0)),
            ],
        ),
        out_shape=[
            jax.ShapeDtypeStruct((slot_count, rank, ff_shard), jnp.float32),
            jax.ShapeDtypeStruct((slot_count, rank, columns - ff_shard), jnp.float32),
        ],
        compiler_params=pltpu.CompilerParams(vmem_limit_bytes=32 * 1024 * 1024),
        cost_estimate=pl.CostEstimate(
            flops=0, bytes_accessed=8 * slot_count * rank * columns, transcendentals=0
        ),
    )(slots, *groups)


def terms_kernel(group_count, out_count, place_ref, *refs):
    dy_refs, refs = refs[:group_count], refs[group_count:]
    *refs, dy_buffer, weight_buffer, total, dy_sems, weight_sems = refs
    weight_refs, out_refs = refs[:-out_count], refs[-out_count:]
    chip, core = place_ref[0], place_ref[1]
    rows_group, depth = dy_refs[0].shape
    step_depth = dy_buffer.shape[-1]
    steps = depth // step_depth
    columns = total.shape[1]

    def start(step):
        slot = lax.rem(step, 2)
        part = pl.ds(pl.multiple_of(step * step_depth, step_depth), step_depth)
        for refs, buffer, sems in (
            (dy_refs, dy_buffer, dy_sems),
            (weight_refs, weight_buffer, weight_sems),
        ):
            row = 0
            for ref in refs:
                rows = pl.ds(row, ref.shape[0])
                pltpu.make_async_copy(
                    ref.at[:, part], buffer.at[slot, rows], sems.at[slot]
                ).start()
                row += ref.shape[0]

    def one_step(step, carry):
        slot = lax.rem(step, 2)

        @pl.when(step + 1 < steps)
        def _():
            start(step + 1)

        for buffer, sems in ((dy_buffer, dy_sems), (weight_buffer, weight_sems)):
            whole = buffer.at[slot]
            pltpu.make_async_copy(whole, whole, sems.at[slot]).wait()
        for column in range(0, columns, 256):
            part = dot_last(dy_buffer[slot], weight_buffer[slot, column : column + 256])
            total[:, column : column + 256] += part
        return carry

    start(jnp.int32(0))
    total[...] = jnp.zeros_like(total)
    lax.fori_loop(0, steps, one_step, 0)
    for group in range(group_count):
        for k in range(4):
            first = group * rows_group + k * TILE

            def tile(first=first):
                return total[first : first + TILE].astype(jnp.bfloat16)

            if out_count == 1:
                out_refs[0][k, group] = tile()
                continue
            x, c = k // 2, k % 2
            slot = jnp.where(chip == x, 1, 0)

            @pl.when(core != c)
            def _(slot=slot, group=group, tile=tile):
                out_refs[0][slot, group] = tile()

            @pl.when(core == c)
            def _(slot=slot, group=group, tile=tile):
                out_refs[1][slot, group] = tile()


def product_terms(groups, weights, place, out_count):
    rows_group, depth = groups[0].shape
    columns = sum(w.shape[0] for w in weights)
    rows = rows_group * len(groups)
    step_depth = 512
    out = jax.ShapeDtypeStruct((4 // out_count, len(groups), TILE, columns), jnp.bfloat16)
    in_hbm = pl.BlockSpec(memory_space=pl.ANY)
    return pl.pallas_call(
        functools.partial(terms_kernel, len(groups), out_count),
        grid_spec=pltpu.PrefetchScalarGridSpec(
            num_scalar_prefetch=1,
            grid=(1,),
            in_specs=[in_hbm] * (len(groups) + len(weights)),
            out_specs=[pl.BlockSpec(out.shape, lambda i, p: (0, 0, 0, 0))] * out_count,
            scratch_shapes=[
                pltpu.VMEM((2, rows, step_depth), jnp.bfloat16),
                pltpu.VMEM((2, columns, step_depth), jnp.bfloat16),
                pltpu.VMEM((rows, columns), jnp.float32),
                pltpu.SemaphoreType.DMA((2,)),
                pltpu.SemaphoreType.DMA((2,)),
            ],
        ),
        out_shape=[out] * out_count,
        compiler_params=pltpu.CompilerParams(vmem_limit_bytes=20 * 1024 * 1024),
        cost_estimate=pl.CostEstimate(flops=0, bytes_accessed=0, transcendentals=0),
    )(place, *groups, *weights)


def after(value, *events):
    return lax.optimization_barrier((value,) + events)[0]


def from_other_core(away):
    return lax.ppermute(away, "tensor", [(0, 1), (1, 0), (2, 3), (3, 2)])


def sum_of_chips(home, got, *events):
    pair = home.astype(jnp.float32) + got.astype(jnp.float32)
    sent = after(pair[0].astype(jnp.bfloat16), *events)
    got = lax.ppermute(sent, "tensor", [(0, 2), (2, 0), (1, 3), (3, 1)])
    return (pair[1] + got.astype(jnp.float32)).astype(jnp.bfloat16)


def sum_by_swap(terms):
    got = lax.all_to_all(terms[0], "tensor", split_axis=0, concat_axis=0, tiled=True)
    return jnp.sum(got.astype(jnp.float32), axis=0).astype(jnp.bfloat16)


PARTNER = [(0, 1), (1, 0), (2, 3), (3, 2)]
MIDDLE = [(1, 2), (2, 1)]
OUTER_TO_MIDDLE = [(0, 2), (3, 1)]
OUTWARD = [(1, 0), (2, 3)]
OTHER_REP = [(0, 1), (1, 0)]
OUTWARD_OTHER_REP = [(4 * r + a, 4 * (1 - r) + b) for r in (0, 1) for a, b in OUTWARD]


def line_of_four(
    tokens,
    grad_out,
    frozen_weight,
    adapter_down,
    adapter_up,
    tenant_ids,
    tenant_token_counts,
    owner_map,
):
    z = lax.axis_index("dp")
    rep = lax.axis_index("rep")
    shard = lax.axis_index("tensor")
    place = jnp.stack([shard // 2, shard % 2]).astype(jnp.int32)
    rows_group, ff_shard = grad_out.shape
    tile_count = rows_group // TILE
    adapter_count, rank = adapter_down.shape[:2]
    slot_count = 2 * adapter_count // 4
    inner = (z == 1) | (z == 2)
    all_tenants = tenant_ids.reshape(-1, TILE)[:, 0]
    tenants = lax.dynamic_slice_in_dim(all_tenants, z * tile_count, tile_count)
    half = frozen_weight.shape[0] // 2

    crossing = lax.dynamic_slice_in_dim(frozen_weight, rep * half, half, 0)
    near = lax.ppermute(crossing, "dp", MIDDLE)
    partner_dy = lax.ppermute(after(grad_out, crossing), "dp", PARTNER)
    other_dy = lax.ppermute(grad_out, "rep", OTHER_REP)

    dy_tiles = grad_out.reshape(tile_count, TILE, ff_shard)
    down_sel = adapter_down[tenants]
    up_sel = adapter_up[tenants]
    own_down = lax.all_to_all(down_sel, "tensor", split_axis=0, concat_axis=2, tiled=True)[0]
    middle = dot_last(own_down, tokens).astype(jnp.bfloat16)
    backed_part = jnp.einsum(
        "krf,ktf->krt", up_sel, dy_tiles, preferred_element_type=jnp.float32
    ).astype(jnp.bfloat16)
    sent = jnp.concatenate([backed_part, jnp.broadcast_to(middle, backed_part.shape)], axis=1)
    got = lax.all_to_all(sent, "tensor", split_axis=0, concat_axis=0, tiled=True)
    backed = jnp.sum(got[:, :rank].astype(jnp.float32), axis=0).astype(jnp.bfloat16)
    middle = got[:, rank:]

    def scale_of(tenants):
        return adapter_scale / tenant_token_counts[tenants].astype(jnp.float32)

    def up_gradients(scale, middle, dy):
        dy = dy.reshape(tile_count, TILE, ff_shard)
        product = jnp.einsum("krt,ktf->krf", middle, dy, preferred_element_type=jnp.float32)
        return (scale[:, None, None] * product).astype(jnp.bfloat16)

    scale = scale_of(tenants)
    tile_up = up_gradients(scale, middle, grad_out)
    own_tile_down = (
        scale[shard] * jnp.dot(backed, tokens, preferred_element_type=jnp.float32)
    ).astype(jnp.bfloat16)
    tile_down = lax.all_to_all(
        own_tile_down, "tensor", split_axis=1, concat_axis=0, tiled=True
    ).reshape(tile_count, rank, -1)
    tile_grads = jnp.concatenate([tile_up, tile_down], axis=2)
    to_partner = jnp.concatenate([middle, tile_down], axis=2)

    from_partner = lax.ppermute(to_partner, "dp", PARTNER)

    partner_index = z + 1 - 2 * (z % 2)
    partner_tenants = lax.dynamic_slice_in_dim(
        all_tenants, partner_index * tile_count, tile_count
    )
    partner_up = up_gradients(
        scale_of(partner_tenants), from_partner[:, :, :TILE], partner_dy
    )
    partner_grads = jnp.concatenate([partner_up, from_partner[:, :, TILE:]], axis=2)
    far = lax.ppermute(after(crossing, partner_grads), "dp", OUTER_TO_MIDDLE)
    partner_other_dy = lax.ppermute(after(partner_dy, other_dy), "rep", OTHER_REP)

    events = (partner_dy, tile_grads, partner_grads)
    own_terms = product_terms([after(grad_out, *events), partner_dy], [frozen_weight], place, 1)
    own_sum = sum_by_swap(own_terms)

    groups = [after(grad_out, near, own_terms[0]), partner_dy, other_dy]
    near_terms = product_terms(groups, [near], place, 1)
    near_sum = sum_by_swap(near_terms)

    near_grads = lax.ppermute(after(tile_grads, near_terms[0]), "dp", MIDDLE)
    far_grads = lax.ppermute(after(partner_grads, near_terms[0]), "dp", MIDDLE)
    partner_block = lax.ppermute(own_sum[1], "dp", PARTNER)

    groups = [after(grad_out, own_sum, near_sum), partner_dy, other_dy]
    far_terms = product_terms(groups, [far], place, 2)
    outer_terms = product_terms(
        [after(partner_other_dy, far_terms[0], near_grads, partner_block)], [near, far], place, 2
    )
    near_grads_out = lax.ppermute(after(near_grads, far_terms[0]), "dp", OUTWARD)
    outer_got = from_other_core(after(outer_terms[0], far_grads))
    far_grads_out = lax.ppermute(far_grads, "dp", OUTWARD)
    far_got = from_other_core(far_terms[0])
    far_sum = sum_of_chips(far_terms[1], far_got)
    outer_sum = sum_of_chips(after(outer_terms[1], near_grads_out), outer_got)[0]
    both_sum = jnp.concatenate([near_sum, far_sum], axis=2)
    both_out = lax.ppermute(both_sum[1], "dp", OUTWARD)
    both_other = lax.ppermute(both_sum[2], "rep", OTHER_REP)
    outer_other = lax.ppermute(
        after(outer_sum, far_grads_out), ("rep", "dp"), OUTWARD_OTHER_REP
    )

    mine = jnp.where(inner, both_sum[0], both_out)
    other = jnp.where(inner, both_other, outer_other)
    low = jnp.where(rep == 0, mine, other)
    high = jnp.where(rep == 0, other, mine)
    near_block = jnp.concatenate([low[:, :half], high[:, :half]], axis=1)
    far_block = jnp.concatenate([low[:, half:], high[:, half:]], axis=1)
    own_block = own_sum[0]

    lora = adapter_scale * lax.dot_general(
        backed, own_down, (((0,), (0,)), ((), ())), preferred_element_type=jnp.float32
    )
    even = z % 2 == 0
    first = jnp.where(even, own_block, partner_block)
    second = jnp.where(even, partner_block, own_block)
    left = z < 2
    frozen = jnp.concatenate(
        [
            jnp.where(left, first, far_block),
            jnp.where(left, second, near_block),
            jnp.where(left, near_block, first),
            jnp.where(left, far_block, second),
        ],
        axis=1,
    )
    input_grad = (frozen.astype(jnp.float32) + lora).astype(jnp.bfloat16)

    near_index = jnp.where(z < 2, 2, 1)
    far_index = jnp.where(z < 2, 3, 0)
    tile_slots = owner_slots(owner_map, slot_count)[all_tenants].reshape(4, tile_count)
    tile_slots = tile_slots - z * slot_count
    nowhere = jnp.full((tile_count,), -1, jnp.int32)
    slots = jnp.concatenate(
        [
            tile_slots[z],
            tile_slots[partner_index],
            jnp.where(inner, tile_slots[near_index], nowhere),
            jnp.where(inner, tile_slots[far_index], nowhere),
            jnp.where(inner, nowhere, tile_slots[near_index]),
            jnp.where(inner, nowhere, tile_slots[far_index]),
        ]
    )
    grad_up, grad_down = place_in_slots(
        [tile_grads, partner_grads, near_grads, far_grads, near_grads_out, far_grads_out],
        slots,
        slot_count,
        ff_shard,
    )
    return input_grad, grad_down, grad_up


def any_line(
    tokens,
    grad_out,
    frozen_weight,
    adapter_down,
    adapter_up,
    tenant_ids,
    tenant_token_counts,
    owner_map,
):
    dp_count = lax.axis_size("dp")
    group_index = lax.axis_index("dp")
    shard_index = lax.axis_index("tensor")
    rows_group, ff_shard = grad_out.shape
    width_shard = adapter_down.shape[2]
    adapter_count = adapter_down.shape[0]
    tile_count = rows_group // TILE
    slot_count = 2 * adapter_count // dp_count
    all_tenants = tenant_ids.reshape(-1, TILE)[:, 0]
    tenants = lax.dynamic_slice_in_dim(all_tenants, group_index * tile_count, tile_count)
    columns = lax.all_to_all(tokens, "tensor", split_axis=1, concat_axis=0, tiled=True)
    down_sel = adapter_down[tenants]
    up_sel = adapter_up[tenants]
    x_tiles = columns.reshape(tile_count, TILE, width_shard)
    dy_tiles = grad_out.reshape(tile_count, TILE, ff_shard)
    middle_part = jnp.einsum("krd,ktd->krt", down_sel, x_tiles, preferred_element_type=jnp.float32)
    backed_part = jnp.einsum("krf,ktf->krt", up_sel, dy_tiles, preferred_element_type=jnp.float32)
    middle = lax.psum(middle_part.astype(jnp.bfloat16), "tensor")
    backed = lax.psum(backed_part.astype(jnp.bfloat16), "tensor")
    whole = lax.all_gather(frozen_weight, "dp", axis=0, tiled=True)
    frozen = dot_last(grad_out, whole).astype(jnp.bfloat16).astype(jnp.float32)
    lora = adapter_scale * jnp.einsum(
        "krt,krd->ktd", backed, down_sel, preferred_element_type=jnp.float32
    ).reshape(rows_group, width_shard)
    start = shard_index * width_shard
    block = lax.dynamic_slice_in_dim(frozen, start, width_shard, 1) + lora
    terms = lax.dynamic_update_slice_in_dim(frozen, block, start, 1).astype(jnp.bfloat16)
    input_grad = lax.psum_scatter(terms, "tensor", scatter_dimension=0, tiled=True)
    scale = (adapter_scale / tenant_token_counts[tenants].astype(jnp.float32))[:, None, None]
    tile_up = scale * jnp.einsum(
        "krt,ktf->krf", middle, dy_tiles, preferred_element_type=jnp.float32
    )
    tile_down = scale * jnp.einsum(
        "krt,ktd->krd", backed, x_tiles, preferred_element_type=jnp.float32
    )
    tile_grads = jnp.concatenate([tile_up, tile_down], axis=2).astype(jnp.bfloat16)
    all_grads = lax.all_gather(tile_grads, "dp", axis=0, tiled=True)
    slots = owner_slots(owner_map, slot_count)[all_tenants] - group_index * slot_count
    grad_up, grad_down = place_in_slots([all_grads], slots, slot_count, ff_shard)
    return input_grad, grad_down, grad_up


def solution(mesh):
    sizes = mesh.shape
    four = sizes["dp"] == 4 and sizes["tensor"] == 4 and sizes["rep"] == 2
    placed = (
        P(("rep", "dp", "tensor"), None),
        P(("rep", "dp"), "tensor"),
        P("dp", "tensor"),
        P("rep", None, "tensor"),
        P("rep", None, "tensor"),
        P("rep"),
        P("rep"),
        P(),
    )
    return jax.shard_map(
        line_of_four if four else any_line,
        mesh=mesh,
        in_specs=placed,
        out_specs=(
            P(("rep", "dp", "tensor"), None),
            P(("rep", "dp"), None, "tensor"),
            P(("rep", "dp"), None, "tensor"),
        ),
        check_vma=False,
    )
```

```python
import functools

import jax
import jax.numpy as jnp
from jax import lax
from jax.experimental import pallas as pl
from jax.experimental.pallas import tpu as pltpu
from jax.sharding import PartitionSpec as P

TILE = 128


adapter_scale = 2.0


def owner_slots(owner_map, slot_count):
    positions = jnp.arange(owner_map.shape[0])
    same_owner = owner_map[:, None] == owner_map[None, :]
    earlier = positions[:, None] > positions[None, :]
    owner_rank = jnp.sum((same_owner & earlier).astype(jnp.int32), axis=1)
    return owner_map * slot_count + owner_rank


def dot_last(a, b):
    return lax.dot_general(a, b, (((1,), (1,)), ((), ())), preferred_element_type=jnp.float32)


def place_kernel(slots_ref, *refs):
    *tile_refs, up_ref, down_ref = refs
    per_step = up_ref.shape[0]
    ff_shard = up_ref.shape[2]
    tiles_each = tile_refs[0].shape[0]
    first = pl.program_id(0) * per_step
    up_ref[...] = jnp.zeros_like(up_ref)
    down_ref[...] = jnp.zeros_like(down_ref)
    for i, tiles_ref in enumerate(tile_refs):
        for k in range(tiles_each):
            local = slots_ref[i * tiles_each + k] - first

            @pl.when((local >= 0) & (local < per_step))
            def _(tiles_ref=tiles_ref, k=k, local=local):
                up_ref[local] += tiles_ref[k, :, :ff_shard].astype(jnp.float32)
                down_ref[local] += tiles_ref[k, :, ff_shard:].astype(jnp.float32)


def place_in_slots(groups, slots, slot_count, ff_shard):
    tile_count, rank, columns = groups[0].shape
    per_step = min(4, slot_count)
    return pl.pallas_call(
        place_kernel,
        grid_spec=pltpu.PrefetchScalarGridSpec(
            num_scalar_prefetch=1,
            grid=(slot_count // per_step,),
            in_specs=[pl.BlockSpec((tile_count, rank, columns), lambda i, s: (0, 0, 0))]
            * len(groups),
            out_specs=[
                pl.BlockSpec((per_step, rank, ff_shard), lambda i, s: (i, 0, 0)),
                pl.BlockSpec((per_step, rank, columns - ff_shard), lambda i, s: (i, 0, 0)),
            ],
        ),
        out_shape=[
            jax.ShapeDtypeStruct((slot_count, rank, ff_shard), jnp.float32),
            jax.ShapeDtypeStruct((slot_count, rank, columns - ff_shard), jnp.float32),
        ],
        compiler_params=pltpu.CompilerParams(vmem_limit_bytes=32 * 1024 * 1024),
        cost_estimate=pl.CostEstimate(
            flops=0, bytes_accessed=8 * slot_count * rank * columns, transcendentals=0
        ),
    )(slots, *groups)


def add_kernel(slots_ref, *refs):
    *tile_refs, _, _, up_ref, down_ref, up_buffer, down_buffer, sems = refs
    slot_count, _, ff_shard = up_ref.shape
    for i, tiles_ref in enumerate(tile_refs):
        copies = []
        for k in range(tiles_ref.shape[0]):
            slot = slots_ref[i * tiles_ref.shape[0] + k]
            hit = (slot >= 0) & (slot < slot_count)
            at = jnp.clip(slot, 0, slot_count - 1)
            pairs = ((up_ref.at[at], up_buffer.at[k]), (down_ref.at[at], down_buffer.at[k]))
            copies.append((hit, pairs, sems.at[k]))
        for hit, pairs, pair_sems in copies:

            @pl.when(hit)
            def _(pairs=pairs, pair_sems=pair_sems):
                for n, (place, buffer) in enumerate(pairs):
                    pltpu.make_async_copy(place, buffer, pair_sems.at[n]).start()

        for k, (hit, pairs, pair_sems) in enumerate(copies):

            @pl.when(hit)
            def _(k=k, pairs=pairs, pair_sems=pair_sems, tiles_ref=tiles_ref):
                for n, (place, buffer) in enumerate(pairs):
                    pltpu.make_async_copy(place, buffer, pair_sems.at[n]).wait()
                up_buffer[k] += tiles_ref[k, :, :ff_shard].astype(jnp.float32)
                down_buffer[k] += tiles_ref[k, :, ff_shard:].astype(jnp.float32)
                for n, (place, buffer) in enumerate(pairs):
                    pltpu.make_async_copy(buffer, place, pair_sems.at[n]).start()

        for hit, pairs, pair_sems in copies:

            @pl.when(hit)
            def _(pairs=pairs, pair_sems=pair_sems):
                for n, (place, buffer) in enumerate(pairs):
                    pltpu.make_async_copy(buffer, place, pair_sems.at[n]).wait()


def add_in_slots(groups, slots, grad_up, grad_down):
    tile_count, rank, columns = groups[0].shape
    ff_shard = grad_up.shape[2]
    in_hbm = pl.BlockSpec(memory_space=pl.ANY)
    whole = pl.BlockSpec((tile_count, rank, columns), lambda i, s: (0, 0, 0))
    return pl.pallas_call(
        add_kernel,
        grid_spec=pltpu.PrefetchScalarGridSpec(
            num_scalar_prefetch=1,
            grid=(1,),
            in_specs=[whole] * len(groups) + [in_hbm, in_hbm],
            out_specs=[in_hbm, in_hbm],
            scratch_shapes=[
                pltpu.VMEM((tile_count, rank, ff_shard), jnp.float32),
                pltpu.VMEM((tile_count, rank, columns - ff_shard), jnp.float32),
                pltpu.SemaphoreType.DMA((tile_count, 2)),
            ],
        ),
        out_shape=[
            jax.ShapeDtypeStruct(grad_up.shape, grad_up.dtype),
            jax.ShapeDtypeStruct(grad_down.shape, grad_down.dtype),
        ],
        input_output_aliases={len(groups) + 1: 0, len(groups) + 2: 1},
        compiler_params=pltpu.CompilerParams(vmem_limit_bytes=20 * 1024 * 1024),
        cost_estimate=pl.CostEstimate(
            flops=0, bytes_accessed=4 * tile_count * rank * columns, transcendentals=0
        ),
    )(slots, *groups, grad_up, grad_down)


def terms_kernel(group_count, out_count, place_ref, *refs):
    dy_refs, refs = refs[:group_count], refs[group_count:]
    *refs, dy_buffer, weight_buffer, total, dy_sems, weight_sems = refs
    weight_refs, out_refs = refs[:-out_count], refs[-out_count:]
    chip, core = place_ref[0], place_ref[1]
    rows_group, depth = dy_refs[0].shape
    step_depth = dy_buffer.shape[-1]
    steps = depth // step_depth
    columns = total.shape[1]

    def start(step):
        slot = lax.rem(step, 2)
        part = pl.ds(pl.multiple_of(step * step_depth, step_depth), step_depth)
        for refs, buffer, sems in (
            (dy_refs, dy_buffer, dy_sems),
            (weight_refs, weight_buffer, weight_sems),
        ):
            row = 0
            for ref in refs:
                rows = pl.ds(row, ref.shape[0])
                pltpu.make_async_copy(
                    ref.at[:, part], buffer.at[slot, rows], sems.at[slot]
                ).start()
                row += ref.shape[0]

    def one_step(step, carry):
        slot = lax.rem(step, 2)

        @pl.when(step + 1 < steps)
        def _():
            start(step + 1)

        for buffer, sems in ((dy_buffer, dy_sems), (weight_buffer, weight_sems)):
            whole = buffer.at[slot]
            pltpu.make_async_copy(whole, whole, sems.at[slot]).wait()
        for column in range(0, columns, 256):
            part = dot_last(dy_buffer[slot], weight_buffer[slot, column : column + 256])
            total[:, column : column + 256] += part
        return carry

    start(jnp.int32(0))
    total[...] = jnp.zeros_like(total)
    lax.fori_loop(0, steps, one_step, 0)
    for group in range(group_count):
        for k in range(4):
            first = group * rows_group + k * TILE

            def tile(first=first):
                return total[first : first + TILE].astype(jnp.bfloat16)

            if out_count == 1:
                out_refs[0][k, group] = tile()
                continue
            x, c = k // 2, k % 2
            slot = jnp.where(chip == x, 1, 0)

            @pl.when(core != c)
            def _(slot=slot, group=group, tile=tile):
                out_refs[0][slot, group] = tile()

            @pl.when(core == c)
            def _(slot=slot, group=group, tile=tile):
                out_refs[1][slot, group] = tile()


def product_terms(groups, weights, place, out_count):
    rows_group, depth = groups[0].shape
    columns = sum(w.shape[0] for w in weights)
    rows = rows_group * len(groups)
    step_depth = 896 if depth % 896 == 0 else depth
    out = jax.ShapeDtypeStruct((4 // out_count, len(groups), TILE, columns), jnp.bfloat16)
    in_hbm = pl.BlockSpec(memory_space=pl.ANY)
    return pl.pallas_call(
        functools.partial(terms_kernel, len(groups), out_count),
        grid_spec=pltpu.PrefetchScalarGridSpec(
            num_scalar_prefetch=1,
            grid=(1,),
            in_specs=[in_hbm] * (len(groups) + len(weights)),
            out_specs=[pl.BlockSpec(out.shape, lambda i, p: (0, 0, 0, 0))] * out_count,
            scratch_shapes=[
                pltpu.VMEM((2, rows, step_depth), jnp.bfloat16),
                pltpu.VMEM((2, columns, step_depth), jnp.bfloat16),
                pltpu.VMEM((rows, columns), jnp.float32),
                pltpu.SemaphoreType.DMA((2,)),
                pltpu.SemaphoreType.DMA((2,)),
            ],
        ),
        out_shape=[out] * out_count,
        compiler_params=pltpu.CompilerParams(vmem_limit_bytes=20 * 1024 * 1024),
        cost_estimate=pl.CostEstimate(flops=0, bytes_accessed=0, transcendentals=0),
    )(place, *groups, *weights)


def after(value, *events):
    return lax.optimization_barrier((value,) + events)[0]


def from_other_core(away):
    return lax.ppermute(away, "tensor", [(0, 1), (1, 0), (2, 3), (3, 2)])


def sum_of_chips(home, got, *events):
    pair = home.astype(jnp.float32) + got.astype(jnp.float32)
    sent = after(pair[0].astype(jnp.bfloat16), *events)
    got = lax.ppermute(sent, "tensor", [(0, 2), (2, 0), (1, 3), (3, 1)])
    return (pair[1] + got.astype(jnp.float32)).astype(jnp.bfloat16)


def sum_by_swap(terms):
    got = lax.all_to_all(terms[0], "tensor", split_axis=0, concat_axis=0, tiled=True)
    return jnp.sum(got.astype(jnp.float32), axis=0).astype(jnp.bfloat16)


PARTNER = [(0, 1), (1, 0), (2, 3), (3, 2)]
MIDDLE = [(1, 2), (2, 1)]
OUTER_TO_MIDDLE = [(0, 2), (3, 1)]
OUTWARD = [(1, 0), (2, 3)]
OTHER_REP = [(0, 1), (1, 0)]
OUTWARD_OTHER_REP = [(4 * r + a, 4 * (1 - r) + b) for r in (0, 1) for a, b in OUTWARD]


def line_of_four(
    tokens,
    grad_out,
    frozen_weight,
    adapter_down,
    adapter_up,
    tenant_ids,
    tenant_token_counts,
    owner_map,
):
    z = lax.axis_index("dp")
    rep = lax.axis_index("rep")
    shard = lax.axis_index("tensor")
    place = jnp.stack([shard // 2, shard % 2]).astype(jnp.int32)
    rows_group, ff_shard = grad_out.shape
    tile_count = rows_group // TILE
    adapter_count, rank = adapter_down.shape[:2]
    slot_count = 2 * adapter_count // 4
    inner = (z == 1) | (z == 2)
    all_tenants = tenant_ids.reshape(-1, TILE)[:, 0]
    tenants = lax.dynamic_slice_in_dim(all_tenants, z * tile_count, tile_count)
    half = frozen_weight.shape[0] // 2

    crossing = lax.dynamic_slice_in_dim(frozen_weight, rep * half, half, 0)
    near = lax.ppermute(crossing, "dp", MIDDLE)
    partner_dy = lax.ppermute(after(grad_out, crossing), "dp", PARTNER)

    dy_tiles = grad_out.reshape(tile_count, TILE, ff_shard)
    down_sel = adapter_down[after(tenants, crossing)]
    other_dy = lax.ppermute(after(grad_out, down_sel), "rep", OTHER_REP)
    up_sel = adapter_up[tenants]
    own_down = lax.all_to_all(down_sel, "tensor", split_axis=0, concat_axis=2, tiled=True)[0]
    middle = dot_last(own_down, tokens).astype(jnp.bfloat16)
    backed_part = jnp.einsum(
        "krf,ktf->krt", up_sel, dy_tiles, preferred_element_type=jnp.float32
    ).astype(jnp.bfloat16)
    sent = jnp.concatenate([backed_part, jnp.broadcast_to(middle, backed_part.shape)], axis=1)
    got = lax.all_to_all(sent, "tensor", split_axis=0, concat_axis=0, tiled=True)
    backed = jnp.sum(got[:, :rank].astype(jnp.float32), axis=0).astype(jnp.bfloat16)
    middle = got[:, rank:]

    def scale_of(tenants):
        return adapter_scale / tenant_token_counts[tenants].astype(jnp.float32)

    def up_gradients(scale, middle, dy):
        dy = dy.reshape(tile_count, TILE, ff_shard)
        product = jnp.einsum("krt,ktf->krf", middle, dy, preferred_element_type=jnp.float32)
        return (scale[:, None, None] * product).astype(jnp.bfloat16)

    scale = scale_of(tenants)
    tile_up = up_gradients(scale, middle, grad_out)
    own_tile_down = (
        scale[shard] * jnp.dot(backed, tokens, preferred_element_type=jnp.float32)
    ).astype(jnp.bfloat16)
    tile_down = lax.all_to_all(
        own_tile_down, "tensor", split_axis=1, concat_axis=0, tiled=True
    ).reshape(tile_count, rank, -1)
    tile_grads = jnp.concatenate([tile_up, tile_down], axis=2)
    to_partner = jnp.concatenate([middle, tile_down], axis=2)

    from_partner = lax.ppermute(to_partner, "dp", PARTNER)

    partner_index = z + 1 - 2 * (z % 2)
    partner_tenants = lax.dynamic_slice_in_dim(
        all_tenants, partner_index * tile_count, tile_count
    )
    partner_up = up_gradients(
        scale_of(partner_tenants), from_partner[:, :, :TILE], partner_dy
    )
    partner_grads = jnp.concatenate([partner_up, from_partner[:, :, TILE:]], axis=2)
    far = lax.ppermute(after(crossing, partner_dy), "dp", OUTER_TO_MIDDLE)
    partner_other_dy = lax.ppermute(partner_dy, "rep", OTHER_REP)

    events = (partner_dy, tile_grads, partner_grads)
    own_terms = product_terms([after(grad_out, *events), partner_dy], [frozen_weight], place, 1)
    own_sum = sum_by_swap(own_terms)

    groups = [after(grad_out, near, own_terms[0]), partner_dy, other_dy]
    near_terms = product_terms(groups, [near], place, 1)
    near_sum = sum_by_swap(near_terms)

    near_grads = lax.ppermute(after(tile_grads, near_terms[0]), "dp", MIDDLE)
    far_grads = lax.ppermute(after(partner_grads, near_terms[0]), "dp", MIDDLE)
    partner_block = lax.ppermute(own_sum[1], "dp", PARTNER)

    tile_slots = owner_slots(owner_map, slot_count)[all_tenants].reshape(4, tile_count)
    tile_slots = tile_slots - z * slot_count
    grad_up, grad_down = place_in_slots(
        [after(tile_grads, near_terms[0]), partner_grads],
        jnp.concatenate([tile_slots[z], tile_slots[partner_index]]),
        slot_count,
        ff_shard,
    )

    groups = [after(grad_out, own_sum, near_sum, grad_up, grad_down), partner_dy, other_dy]
    far_terms = product_terms(groups, [far], place, 2)
    outer_terms = product_terms(
        [after(partner_other_dy, far_terms[0], near_grads, partner_block)], [near, far], place, 2
    )
    near_grads_out = lax.ppermute(after(near_grads, far_terms[0]), "dp", OUTWARD)
    outer_got = from_other_core(after(outer_terms[0], far_grads))
    far_grads_out = lax.ppermute(far_grads, "dp", OUTWARD)
    far_got = from_other_core(far_terms[0])
    far_sum = sum_of_chips(far_terms[1], far_got)
    outer_sum = sum_of_chips(after(outer_terms[1], near_grads_out), outer_got)[0]
    both_sum = jnp.concatenate([near_sum, far_sum], axis=2)
    both_out = lax.ppermute(after(both_sum[1], far_grads_out), "dp", OUTWARD)
    both_other = lax.ppermute(both_sum[2], "rep", OTHER_REP)
    outer_other = lax.ppermute(outer_sum, ("rep", "dp"), OUTWARD_OTHER_REP)

    mine = jnp.where(inner, both_sum[0], both_out)
    other = jnp.where(inner, both_other, outer_other)
    low = jnp.where(rep == 0, mine, other)
    high = jnp.where(rep == 0, other, mine)
    near_block = jnp.concatenate([low[:, :half], high[:, :half]], axis=1)
    far_block = jnp.concatenate([low[:, half:], high[:, half:]], axis=1)
    own_block = own_sum[0]

    lora = adapter_scale * lax.dot_general(
        backed, own_down, (((0,), (0,)), ((), ())), preferred_element_type=jnp.float32
    )
    even = z % 2 == 0
    first = jnp.where(even, own_block, partner_block)
    second = jnp.where(even, partner_block, own_block)
    left = z < 2
    frozen = jnp.concatenate(
        [
            jnp.where(left, first, far_block),
            jnp.where(left, second, near_block),
            jnp.where(left, near_block, first),
            jnp.where(left, far_block, second),
        ],
        axis=1,
    )
    input_grad = (frozen.astype(jnp.float32) + lora).astype(jnp.bfloat16)

    near_index = jnp.where(z < 2, 2, 1)
    far_index = jnp.where(z < 2, 3, 0)
    nowhere = jnp.full((tile_count,), -1, jnp.int32)
    slots = jnp.concatenate(
        [
            jnp.where(inner, tile_slots[near_index], nowhere),
            jnp.where(inner, nowhere, tile_slots[near_index]),
            jnp.where(inner, tile_slots[far_index], nowhere),
            jnp.where(inner, nowhere, tile_slots[far_index]),
        ]
    )
    grad_up, grad_down = add_in_slots(
        [near_grads, near_grads_out, far_grads, far_grads_out], slots, grad_up, grad_down
    )
    return input_grad, grad_down, grad_up


def any_line(
    tokens,
    grad_out,
    frozen_weight,
    adapter_down,
    adapter_up,
    tenant_ids,
    tenant_token_counts,
    owner_map,
):
    dp_count = lax.axis_size("dp")
    group_index = lax.axis_index("dp")
    shard_index = lax.axis_index("tensor")
    rows_group, ff_shard = grad_out.shape
    width_shard = adapter_down.shape[2]
    adapter_count = adapter_down.shape[0]
    tile_count = rows_group // TILE
    slot_count = 2 * adapter_count // dp_count
    all_tenants = tenant_ids.reshape(-1, TILE)[:, 0]
    tenants = lax.dynamic_slice_in_dim(all_tenants, group_index * tile_count, tile_count)
    columns = lax.all_to_all(tokens, "tensor", split_axis=1, concat_axis=0, tiled=True)
    down_sel = adapter_down[tenants]
    up_sel = adapter_up[tenants]
    x_tiles = columns.reshape(tile_count, TILE, width_shard)
    dy_tiles = grad_out.reshape(tile_count, TILE, ff_shard)
    middle_part = jnp.einsum("krd,ktd->krt", down_sel, x_tiles, preferred_element_type=jnp.float32)
    backed_part = jnp.einsum("krf,ktf->krt", up_sel, dy_tiles, preferred_element_type=jnp.float32)
    middle = lax.psum(middle_part.astype(jnp.bfloat16), "tensor")
    backed = lax.psum(backed_part.astype(jnp.bfloat16), "tensor")
    whole = lax.all_gather(frozen_weight, "dp", axis=0, tiled=True)
    frozen = dot_last(grad_out, whole).astype(jnp.bfloat16).astype(jnp.float32)
    lora = adapter_scale * jnp.einsum(
        "krt,krd->ktd", backed, down_sel, preferred_element_type=jnp.float32
    ).reshape(rows_group, width_shard)
    start = shard_index * width_shard
    block = lax.dynamic_slice_in_dim(frozen, start, width_shard, 1) + lora
    terms = lax.dynamic_update_slice_in_dim(frozen, block, start, 1).astype(jnp.bfloat16)
    input_grad = lax.psum_scatter(terms, "tensor", scatter_dimension=0, tiled=True)
    scale = (adapter_scale / tenant_token_counts[tenants].astype(jnp.float32))[:, None, None]
    tile_up = scale * jnp.einsum(
        "krt,ktf->krf", middle, dy_tiles, preferred_element_type=jnp.float32
    )
    tile_down = scale * jnp.einsum(
        "krt,ktd->krd", backed, x_tiles, preferred_element_type=jnp.float32
    )
    tile_grads = jnp.concatenate([tile_up, tile_down], axis=2).astype(jnp.bfloat16)
    all_grads = lax.all_gather(tile_grads, "dp", axis=0, tiled=True)
    slots = owner_slots(owner_map, slot_count)[all_tenants] - group_index * slot_count
    grad_up, grad_down = place_in_slots([all_grads], slots, slot_count, ff_shard)
    return input_grad, grad_down, grad_up


def solution(mesh):
    sizes = mesh.shape
    four = sizes["dp"] == 4 and sizes["tensor"] == 4 and sizes["rep"] == 2
    placed = (
        P(("rep", "dp", "tensor"), None),
        P(("rep", "dp"), "tensor"),
        P("dp", "tensor"),
        P("rep", None, "tensor"),
        P("rep", None, "tensor"),
        P("rep"),
        P("rep"),
        P(),
    )
    return jax.shard_map(
        line_of_four if four else any_line,
        mesh=mesh,
        in_specs=placed,
        out_specs=(
            P(("rep", "dp", "tensor"), None),
            P(("rep", "dp"), None, "tensor"),
            P(("rep", "dp"), None, "tensor"),
        ),
        check_vma=False,
    )
```

```python
import functools

import jax
import jax.numpy as jnp
from jax import lax
from jax.experimental import pallas as pl
from jax.experimental.pallas import tpu as pltpu
from jax.sharding import PartitionSpec as P

TILE = 128


adapter_scale = 2.0


def owner_slots(owner_map, slot_count):
    positions = jnp.arange(owner_map.shape[0])
    same_owner = owner_map[:, None] == owner_map[None, :]
    earlier = positions[:, None] > positions[None, :]
    owner_rank = jnp.sum((same_owner & earlier).astype(jnp.int32), axis=1)
    return owner_map * slot_count + owner_rank


def dot_last(a, b):
    return lax.dot_general(a, b, (((1,), (1,)), ((), ())), preferred_element_type=jnp.float32)


def place_kernel(slots_ref, *refs):
    *tile_refs, up_ref, down_ref = refs
    per_step = up_ref.shape[0]
    ff_shard = up_ref.shape[2]
    tiles_each = tile_refs[0].shape[0]
    first = pl.program_id(0) * per_step
    up_ref[...] = jnp.zeros_like(up_ref)
    down_ref[...] = jnp.zeros_like(down_ref)
    for i, tiles_ref in enumerate(tile_refs):
        for k in range(tiles_each):
            local = slots_ref[i * tiles_each + k] - first

            @pl.when((local >= 0) & (local < per_step))
            def _(tiles_ref=tiles_ref, k=k, local=local):
                up_ref[local] += tiles_ref[k, :, :ff_shard].astype(jnp.float32)
                down_ref[local] += tiles_ref[k, :, ff_shard:].astype(jnp.float32)


def place_in_slots(groups, slots, slot_count, ff_shard):
    tile_count, rank, columns = groups[0].shape
    per_step = min(4, slot_count)
    return pl.pallas_call(
        place_kernel,
        grid_spec=pltpu.PrefetchScalarGridSpec(
            num_scalar_prefetch=1,
            grid=(slot_count // per_step,),
            in_specs=[pl.BlockSpec((tile_count, rank, columns), lambda i, s: (0, 0, 0))]
            * len(groups),
            out_specs=[
                pl.BlockSpec((per_step, rank, ff_shard), lambda i, s: (i, 0, 0)),
                pl.BlockSpec((per_step, rank, columns - ff_shard), lambda i, s: (i, 0, 0)),
            ],
        ),
        out_shape=[
            jax.ShapeDtypeStruct((slot_count, rank, ff_shard), jnp.float32),
            jax.ShapeDtypeStruct((slot_count, rank, columns - ff_shard), jnp.float32),
        ],
        compiler_params=pltpu.CompilerParams(vmem_limit_bytes=32 * 1024 * 1024),
        cost_estimate=pl.CostEstimate(
            flops=0, bytes_accessed=8 * slot_count * rank * columns, transcendentals=0
        ),
    )(slots, *groups)


def add_kernel(slots_ref, *refs):
    *tile_refs, _, _, up_ref, down_ref, up_buffer, down_buffer, sems = refs
    slot_count, _, ff_shard = up_ref.shape
    for i, tiles_ref in enumerate(tile_refs):
        copies = []
        for k in range(tiles_ref.shape[0]):
            slot = slots_ref[i * tiles_ref.shape[0] + k]
            hit = (slot >= 0) & (slot < slot_count)
            at = jnp.clip(slot, 0, slot_count - 1)
            pairs = ((up_ref.at[at], up_buffer.at[k]), (down_ref.at[at], down_buffer.at[k]))
            copies.append((hit, pairs, sems.at[k]))
        for hit, pairs, pair_sems in copies:

            @pl.when(hit)
            def _(pairs=pairs, pair_sems=pair_sems):
                for n, (place, buffer) in enumerate(pairs):
                    pltpu.make_async_copy(place, buffer, pair_sems.at[n]).start()

        for k, (hit, pairs, pair_sems) in enumerate(copies):

            @pl.when(hit)
            def _(k=k, pairs=pairs, pair_sems=pair_sems, tiles_ref=tiles_ref):
                for n, (place, buffer) in enumerate(pairs):
                    pltpu.make_async_copy(place, buffer, pair_sems.at[n]).wait()
                up_buffer[k] += tiles_ref[k, :, :ff_shard].astype(jnp.float32)
                down_buffer[k] += tiles_ref[k, :, ff_shard:].astype(jnp.float32)
                for n, (place, buffer) in enumerate(pairs):
                    pltpu.make_async_copy(buffer, place, pair_sems.at[n]).start()

        for hit, pairs, pair_sems in copies:

            @pl.when(hit)
            def _(pairs=pairs, pair_sems=pair_sems):
                for n, (place, buffer) in enumerate(pairs):
                    pltpu.make_async_copy(buffer, place, pair_sems.at[n]).wait()


def add_in_slots(groups, slots, grad_up, grad_down):
    tile_count, rank, columns = groups[0].shape
    ff_shard = grad_up.shape[2]
    in_hbm = pl.BlockSpec(memory_space=pl.ANY)
    whole = pl.BlockSpec((tile_count, rank, columns), lambda i, s: (0, 0, 0))
    return pl.pallas_call(
        add_kernel,
        grid_spec=pltpu.PrefetchScalarGridSpec(
            num_scalar_prefetch=1,
            grid=(1,),
            in_specs=[whole] * len(groups) + [in_hbm, in_hbm],
            out_specs=[in_hbm, in_hbm],
            scratch_shapes=[
                pltpu.VMEM((tile_count, rank, ff_shard), jnp.float32),
                pltpu.VMEM((tile_count, rank, columns - ff_shard), jnp.float32),
                pltpu.SemaphoreType.DMA((tile_count, 2)),
            ],
        ),
        out_shape=[
            jax.ShapeDtypeStruct(grad_up.shape, grad_up.dtype),
            jax.ShapeDtypeStruct(grad_down.shape, grad_down.dtype),
        ],
        input_output_aliases={len(groups) + 1: 0, len(groups) + 2: 1},
        compiler_params=pltpu.CompilerParams(vmem_limit_bytes=20 * 1024 * 1024),
        cost_estimate=pl.CostEstimate(
            flops=0, bytes_accessed=4 * tile_count * rank * columns, transcendentals=0
        ),
    )(slots, *groups, grad_up, grad_down)


def terms_kernel(group_count, out_count, place_ref, *refs):
    dy_refs, refs = refs[:group_count], refs[group_count:]
    *refs, dy_buffer, weight_buffer, total, dy_sems, weight_sems = refs
    weight_refs, out_refs = refs[:-out_count], refs[-out_count:]
    chip, core = place_ref[0], place_ref[1]
    rows_group, depth = dy_refs[0].shape
    step_depth = dy_buffer.shape[-1]
    steps = depth // step_depth
    columns = total.shape[1]

    def start(step):
        slot = lax.rem(step, 2)
        part = pl.ds(pl.multiple_of(step * step_depth, step_depth), step_depth)
        for refs, buffer, sems in (
            (dy_refs, dy_buffer, dy_sems),
            (weight_refs, weight_buffer, weight_sems),
        ):
            row = 0
            for ref in refs:
                rows = pl.ds(row, ref.shape[0])
                pltpu.make_async_copy(
                    ref.at[:, part], buffer.at[slot, rows], sems.at[slot]
                ).start()
                row += ref.shape[0]

    def one_step(step, carry):
        slot = lax.rem(step, 2)

        @pl.when(step + 1 < steps)
        def _():
            start(step + 1)

        for buffer, sems in ((dy_buffer, dy_sems), (weight_buffer, weight_sems)):
            whole = buffer.at[slot]
            pltpu.make_async_copy(whole, whole, sems.at[slot]).wait()
        for column in range(0, columns, 256):
            part = dot_last(dy_buffer[slot], weight_buffer[slot, column : column + 256])
            total[:, column : column + 256] += part
        return carry

    start(jnp.int32(0))
    total[...] = jnp.zeros_like(total)
    lax.fori_loop(0, steps, one_step, 0)
    for group in range(group_count):
        for k in range(4):
            first = group * rows_group + k * TILE

            def tile(first=first):
                return total[first : first + TILE].astype(jnp.bfloat16)

            if out_count == 1:
                out_refs[0][k, group] = tile()
                continue
            x, c = k // 2, k % 2
            slot = jnp.where(chip == x, 1, 0)

            @pl.when(core != c)
            def _(slot=slot, group=group, tile=tile):
                out_refs[0][slot, group] = tile()

            @pl.when(core == c)
            def _(slot=slot, group=group, tile=tile):
                out_refs[1][slot, group] = tile()


def product_terms(groups, weights, place, out_count):
    rows_group, depth = groups[0].shape
    columns = sum(w.shape[0] for w in weights)
    rows = rows_group * len(groups)
    step_depth = 896 if depth % 896 == 0 else depth
    out = jax.ShapeDtypeStruct((4 // out_count, len(groups), TILE, columns), jnp.bfloat16)
    in_hbm = pl.BlockSpec(memory_space=pl.ANY)
    return pl.pallas_call(
        functools.partial(terms_kernel, len(groups), out_count),
        grid_spec=pltpu.PrefetchScalarGridSpec(
            num_scalar_prefetch=1,
            grid=(1,),
            in_specs=[in_hbm] * (len(groups) + len(weights)),
            out_specs=[pl.BlockSpec(out.shape, lambda i, p: (0, 0, 0, 0))] * out_count,
            scratch_shapes=[
                pltpu.VMEM((2, rows, step_depth), jnp.bfloat16),
                pltpu.VMEM((2, columns, step_depth), jnp.bfloat16),
                pltpu.VMEM((rows, columns), jnp.float32),
                pltpu.SemaphoreType.DMA((2,)),
                pltpu.SemaphoreType.DMA((2,)),
            ],
        ),
        out_shape=[out] * out_count,
        compiler_params=pltpu.CompilerParams(vmem_limit_bytes=20 * 1024 * 1024),
        cost_estimate=pl.CostEstimate(flops=0, bytes_accessed=0, transcendentals=0),
    )(place, *groups, *weights)


def assemble_kernel(flags_ref, *refs):
    own_ref, partner_ref, here_ref, out_ref, swapped_ref, diagonal_ref = refs[:6]
    backed_ref, down_ref, input_grad_ref, lora = refs[6:]
    z, rep = flags_ref[0], flags_ref[1]
    width = own_ref.shape[1]
    half = width // 2
    lora[...] = adapter_scale * lax.dot_general(
        backed_ref[...],
        down_ref[...],
        (((0,), (0,)), ((), ())),
        preferred_element_type=jnp.float32,
    )
    inner = (z == 1) | (z == 2)
    near_block = jnp.where(z < 2, 2, 1)
    far_block = jnp.where(z < 2, 3, 0)

    def put(start, values):
        columns = pl.ds(pl.multiple_of(start, half), values.shape[1])
        input_grad_ref[:, columns] = (values.astype(jnp.float32) + lora[:, columns]).astype(
            input_grad_ref.dtype
        )

    put(z * width, own_ref[...])
    put((z + 1 - 2 * lax.rem(z, 2)) * width, partner_ref[...])
    for block, columns in ((near_block, slice(0, half)), (far_block, slice(half, width))):
        mine = jnp.where(inner, here_ref[:, columns], out_ref[:, columns])
        put(block * width + rep * half, mine)
        other = jnp.where(inner, swapped_ref[:, columns], diagonal_ref[:, columns])
        put(block * width + (1 - rep) * half, other)


def assemble(z, rep, blocks, backed, own_down):
    whole = [pl.BlockSpec(x.shape, lambda i, f: (0, 0)) for x in (*blocks, backed, own_down)]
    shape = (blocks[0].shape[0], own_down.shape[1])
    return pl.pallas_call(
        assemble_kernel,
        grid_spec=pltpu.PrefetchScalarGridSpec(
            num_scalar_prefetch=1,
            grid=(1,),
            in_specs=whole,
            out_specs=pl.BlockSpec(shape, lambda i, f: (0, 0)),
            scratch_shapes=[pltpu.VMEM(shape, jnp.float32)],
        ),
        out_shape=jax.ShapeDtypeStruct(shape, jnp.bfloat16),
        compiler_params=pltpu.CompilerParams(vmem_limit_bytes=20 * 1024 * 1024),
        cost_estimate=pl.CostEstimate(flops=0, bytes_accessed=0, transcendentals=0),
    )(jnp.stack([z, rep]).astype(jnp.int32), *blocks, backed, own_down)


def after(value, *events):
    return lax.optimization_barrier((value,) + events)[0]


def from_other_core(away):
    return lax.ppermute(away, "tensor", [(0, 1), (1, 0), (2, 3), (3, 2)])


def sum_of_chips(home, got, *events):
    pair = home.astype(jnp.float32) + got.astype(jnp.float32)
    sent = after(pair[0].astype(jnp.bfloat16), *events)
    got = lax.ppermute(sent, "tensor", [(0, 2), (2, 0), (1, 3), (3, 1)])
    return (pair[1] + got.astype(jnp.float32)).astype(jnp.bfloat16)


def sum_by_swap(terms):
    got = lax.all_to_all(terms[0], "tensor", split_axis=0, concat_axis=0, tiled=True)
    return jnp.sum(got.astype(jnp.float32), axis=0).astype(jnp.bfloat16)


PARTNER = [(0, 1), (1, 0), (2, 3), (3, 2)]
MIDDLE = [(1, 2), (2, 1)]
OUTER_TO_MIDDLE = [(0, 2), (3, 1)]
OUTWARD = [(1, 0), (2, 3)]
OTHER_REP = [(0, 1), (1, 0)]
OUTWARD_OTHER_REP = [(4 * r + a, 4 * (1 - r) + b) for r in (0, 1) for a, b in OUTWARD]


def line_of_four(
    tokens,
    grad_out,
    frozen_weight,
    adapter_down,
    adapter_up,
    tenant_ids,
    tenant_token_counts,
    owner_map,
):
    z = lax.axis_index("dp")
    rep = lax.axis_index("rep")
    shard = lax.axis_index("tensor")
    place = jnp.stack([shard // 2, shard % 2]).astype(jnp.int32)
    rows_group, ff_shard = grad_out.shape
    tile_count = rows_group // TILE
    adapter_count, rank = adapter_down.shape[:2]
    slot_count = 2 * adapter_count // 4
    inner = (z == 1) | (z == 2)
    all_tenants = tenant_ids.reshape(-1, TILE)[:, 0]
    tenants = lax.dynamic_slice_in_dim(all_tenants, z * tile_count, tile_count)
    half = frozen_weight.shape[0] // 2

    crossing = lax.dynamic_slice_in_dim(frozen_weight, rep * half, half, 0)
    near = lax.ppermute(crossing, "dp", MIDDLE)
    partner_dy = lax.ppermute(after(grad_out, crossing), "dp", PARTNER)

    dy_tiles = grad_out.reshape(tile_count, TILE, ff_shard)
    down_sel = adapter_down[after(tenants, crossing)]
    other_dy = lax.ppermute(after(grad_out, down_sel), "rep", OTHER_REP)
    up_sel = adapter_up[tenants]
    own_down = lax.all_to_all(down_sel, "tensor", split_axis=0, concat_axis=2, tiled=True)[0]
    middle = dot_last(own_down, tokens).astype(jnp.bfloat16)
    backed_part = jnp.einsum(
        "krf,ktf->krt", up_sel, dy_tiles, preferred_element_type=jnp.float32
    ).astype(jnp.bfloat16)
    sent = jnp.concatenate([backed_part, jnp.broadcast_to(middle, backed_part.shape)], axis=1)
    got = lax.all_to_all(sent, "tensor", split_axis=0, concat_axis=0, tiled=True)
    backed = jnp.sum(got[:, :rank].astype(jnp.float32), axis=0).astype(jnp.bfloat16)
    middle = got[:, rank:]

    def scale_of(tenants):
        return adapter_scale / tenant_token_counts[tenants].astype(jnp.float32)

    def up_gradients(scale, middle, dy):
        dy = dy.reshape(tile_count, TILE, ff_shard)
        product = jnp.einsum("krt,ktf->krf", middle, dy, preferred_element_type=jnp.float32)
        return (scale[:, None, None] * product).astype(jnp.bfloat16)

    scale = scale_of(tenants)
    tile_up = up_gradients(scale, middle, grad_out)
    own_tile_down = (
        scale[shard] * jnp.dot(backed, tokens, preferred_element_type=jnp.float32)
    ).astype(jnp.bfloat16)
    tile_down = lax.all_to_all(
        own_tile_down, "tensor", split_axis=1, concat_axis=0, tiled=True
    ).reshape(tile_count, rank, -1)
    tile_grads = jnp.concatenate([tile_up, tile_down], axis=2)
    to_partner = jnp.concatenate([middle, tile_down], axis=2)

    from_partner = lax.ppermute(to_partner, "dp", PARTNER)

    partner_index = z + 1 - 2 * (z % 2)
    partner_tenants = lax.dynamic_slice_in_dim(
        all_tenants, partner_index * tile_count, tile_count
    )
    partner_up = up_gradients(
        scale_of(partner_tenants), from_partner[:, :, :TILE], partner_dy
    )
    partner_grads = jnp.concatenate([partner_up, from_partner[:, :, TILE:]], axis=2)
    far = lax.ppermute(after(crossing, partner_dy), "dp", OUTER_TO_MIDDLE)
    partner_other_dy = lax.ppermute(partner_dy, "rep", OTHER_REP)

    events = (partner_dy, tile_grads, partner_grads)
    own_terms = product_terms([after(grad_out, *events), partner_dy], [frozen_weight], place, 1)
    own_sum = sum_by_swap(own_terms)

    groups = [after(grad_out, near, own_terms[0]), partner_dy, other_dy]
    near_terms = product_terms(groups, [near], place, 1)
    near_sum = sum_by_swap(near_terms)

    near_grads = lax.ppermute(after(tile_grads, near_terms[0]), "dp", MIDDLE)
    far_grads = lax.ppermute(after(partner_grads, own_sum), "dp", MIDDLE)
    partner_block = lax.ppermute(own_sum[1], "dp", PARTNER)

    tile_slots = owner_slots(owner_map, slot_count)[all_tenants].reshape(4, tile_count)
    tile_slots = tile_slots - z * slot_count
    grad_up, grad_down = place_in_slots(
        [after(tile_grads, near_terms[0]), partner_grads],
        jnp.concatenate([tile_slots[z], tile_slots[partner_index]]),
        slot_count,
        ff_shard,
    )

    groups = [after(grad_out, own_sum, near_sum, grad_up, grad_down), partner_dy, other_dy]
    far_terms = product_terms(groups, [far], place, 2)
    outer_terms = product_terms(
        [after(partner_other_dy, far_terms[0], near_grads, partner_block)], [near, far], place, 2
    )
    near_grads_out = lax.ppermute(after(near_grads, far_terms[0]), "dp", OUTWARD)
    outer_got = from_other_core(after(outer_terms[0], far_grads))
    far_grads_out = lax.ppermute(far_grads, "dp", OUTWARD)
    far_got = from_other_core(far_terms[0])
    far_sum = sum_of_chips(far_terms[1], far_got)
    outer_sum = sum_of_chips(after(outer_terms[1], near_grads_out), outer_got)[0]
    both_sum = jnp.concatenate([near_sum, far_sum], axis=2)
    both_out = lax.ppermute(both_sum[1], "dp", OUTWARD)
    both_other = lax.ppermute(both_sum[2], "rep", OTHER_REP)
    outer_other = lax.ppermute(
        after(outer_sum, far_grads_out), ("rep", "dp"), OUTWARD_OTHER_REP
    )

    blocks = [own_sum[0], partner_block, both_sum[0], both_out, both_other, outer_other]
    input_grad = assemble(z, rep, blocks, backed, own_down)

    near_index = jnp.where(z < 2, 2, 1)
    far_index = jnp.where(z < 2, 3, 0)
    nowhere = jnp.full((tile_count,), -1, jnp.int32)
    slots = jnp.concatenate(
        [
            jnp.where(inner, tile_slots[near_index], nowhere),
            jnp.where(inner, nowhere, tile_slots[near_index]),
            jnp.where(inner, tile_slots[far_index], nowhere),
            jnp.where(inner, nowhere, tile_slots[far_index]),
        ]
    )
    grad_up, grad_down = add_in_slots(
        [near_grads, near_grads_out, far_grads, far_grads_out], slots, grad_up, grad_down
    )
    return input_grad, grad_down, grad_up


def any_line(
    tokens,
    grad_out,
    frozen_weight,
    adapter_down,
    adapter_up,
    tenant_ids,
    tenant_token_counts,
    owner_map,
):
    dp_count = lax.axis_size("dp")
    group_index = lax.axis_index("dp")
    shard_index = lax.axis_index("tensor")
    rows_group, ff_shard = grad_out.shape
    width_shard = adapter_down.shape[2]
    adapter_count = adapter_down.shape[0]
    tile_count = rows_group // TILE
    slot_count = 2 * adapter_count // dp_count
    all_tenants = tenant_ids.reshape(-1, TILE)[:, 0]
    tenants = lax.dynamic_slice_in_dim(all_tenants, group_index * tile_count, tile_count)
    columns = lax.all_to_all(tokens, "tensor", split_axis=1, concat_axis=0, tiled=True)
    down_sel = adapter_down[tenants]
    up_sel = adapter_up[tenants]
    x_tiles = columns.reshape(tile_count, TILE, width_shard)
    dy_tiles = grad_out.reshape(tile_count, TILE, ff_shard)
    middle_part = jnp.einsum("krd,ktd->krt", down_sel, x_tiles, preferred_element_type=jnp.float32)
    backed_part = jnp.einsum("krf,ktf->krt", up_sel, dy_tiles, preferred_element_type=jnp.float32)
    middle = lax.psum(middle_part.astype(jnp.bfloat16), "tensor")
    backed = lax.psum(backed_part.astype(jnp.bfloat16), "tensor")
    whole = lax.all_gather(frozen_weight, "dp", axis=0, tiled=True)
    frozen = dot_last(grad_out, whole).astype(jnp.bfloat16).astype(jnp.float32)
    lora = adapter_scale * jnp.einsum(
        "krt,krd->ktd", backed, down_sel, preferred_element_type=jnp.float32
    ).reshape(rows_group, width_shard)
    start = shard_index * width_shard
    block = lax.dynamic_slice_in_dim(frozen, start, width_shard, 1) + lora
    terms = lax.dynamic_update_slice_in_dim(frozen, block, start, 1).astype(jnp.bfloat16)
    input_grad = lax.psum_scatter(terms, "tensor", scatter_dimension=0, tiled=True)
    scale = (adapter_scale / tenant_token_counts[tenants].astype(jnp.float32))[:, None, None]
    tile_up = scale * jnp.einsum(
        "krt,ktf->krf", middle, dy_tiles, preferred_element_type=jnp.float32
    )
    tile_down = scale * jnp.einsum(
        "krt,ktd->krd", backed, x_tiles, preferred_element_type=jnp.float32
    )
    tile_grads = jnp.concatenate([tile_up, tile_down], axis=2).astype(jnp.bfloat16)
    all_grads = lax.all_gather(tile_grads, "dp", axis=0, tiled=True)
    slots = owner_slots(owner_map, slot_count)[all_tenants] - group_index * slot_count
    grad_up, grad_down = place_in_slots([all_grads], slots, slot_count, ff_shard)
    return input_grad, grad_down, grad_up


def solution(mesh):
    sizes = mesh.shape
    four = sizes["dp"] == 4 and sizes["tensor"] == 4 and sizes["rep"] == 2
    placed = (
        P(("rep", "dp", "tensor"), None),
        P(("rep", "dp"), "tensor"),
        P("dp", "tensor"),
        P("rep", None, "tensor"),
        P("rep", None, "tensor"),
        P("rep"),
        P("rep"),
        P(),
    )
    return jax.shard_map(
        line_of_four if four else any_line,
        mesh=mesh,
        in_specs=placed,
        out_specs=(
            P(("rep", "dp", "tensor"), None),
            P(("rep", "dp"), None, "tensor"),
            P(("rep", "dp"), None, "tensor"),
        ),
        check_vma=False,
    )
```

```python
import functools

import jax
import jax.numpy as jnp
from jax import lax
from jax.experimental import pallas as pl
from jax.experimental.pallas import tpu as pltpu
from jax.sharding import PartitionSpec as P

TILE = 128


adapter_scale = 2.0


def owner_slots(owner_map, slot_count):
    positions = jnp.arange(owner_map.shape[0])
    same_owner = owner_map[:, None] == owner_map[None, :]
    earlier = positions[:, None] > positions[None, :]
    owner_rank = jnp.sum((same_owner & earlier).astype(jnp.int32), axis=1)
    return owner_map * slot_count + owner_rank


def dot_last(a, b):
    return lax.dot_general(a, b, (((1,), (1,)), ((), ())), preferred_element_type=jnp.float32)


def place_kernel(slots_ref, *refs):
    *tile_refs, up_ref, down_ref = refs
    per_step = up_ref.shape[0]
    ff_shard = up_ref.shape[2]
    tiles_each = tile_refs[0].shape[0]
    first = pl.program_id(0) * per_step
    up_ref[...] = jnp.zeros_like(up_ref)
    down_ref[...] = jnp.zeros_like(down_ref)
    for i, tiles_ref in enumerate(tile_refs):
        for k in range(tiles_each):
            local = slots_ref[i * tiles_each + k] - first

            @pl.when((local >= 0) & (local < per_step))
            def _(tiles_ref=tiles_ref, k=k, local=local):
                up_ref[local] += tiles_ref[k, :, :ff_shard].astype(jnp.float32)
                down_ref[local] += tiles_ref[k, :, ff_shard:].astype(jnp.float32)


def place_in_slots(groups, slots, slot_count, ff_shard):
    tile_count, rank, columns = groups[0].shape
    per_step = min(4, slot_count)
    return pl.pallas_call(
        place_kernel,
        grid_spec=pltpu.PrefetchScalarGridSpec(
            num_scalar_prefetch=1,
            grid=(slot_count // per_step,),
            in_specs=[pl.BlockSpec((tile_count, rank, columns), lambda i, s: (0, 0, 0))]
            * len(groups),
            out_specs=[
                pl.BlockSpec((per_step, rank, ff_shard), lambda i, s: (i, 0, 0)),
                pl.BlockSpec((per_step, rank, columns - ff_shard), lambda i, s: (i, 0, 0)),
            ],
        ),
        out_shape=[
            jax.ShapeDtypeStruct((slot_count, rank, ff_shard), jnp.float32),
            jax.ShapeDtypeStruct((slot_count, rank, columns - ff_shard), jnp.float32),
        ],
        compiler_params=pltpu.CompilerParams(vmem_limit_bytes=32 * 1024 * 1024),
        cost_estimate=pl.CostEstimate(
            flops=0, bytes_accessed=8 * slot_count * rank * columns, transcendentals=0
        ),
    )(slots, *groups)


def add_kernel(slots_ref, *refs):
    *tile_refs, _, _, up_ref, down_ref, up_buffer, down_buffer, sems = refs
    slot_count, _, ff_shard = up_ref.shape
    for i, tiles_ref in enumerate(tile_refs):
        copies = []
        for k in range(tiles_ref.shape[0]):
            slot = slots_ref[i * tiles_ref.shape[0] + k]
            hit = (slot >= 0) & (slot < slot_count)
            at = jnp.clip(slot, 0, slot_count - 1)
            pairs = ((up_ref.at[at], up_buffer.at[k]), (down_ref.at[at], down_buffer.at[k]))
            copies.append((hit, pairs, sems.at[k]))
        for hit, pairs, pair_sems in copies:

            @pl.when(hit)
            def _(pairs=pairs, pair_sems=pair_sems):
                for n, (place, buffer) in enumerate(pairs):
                    pltpu.make_async_copy(place, buffer, pair_sems.at[n]).start()

        for k, (hit, pairs, pair_sems) in enumerate(copies):

            @pl.when(hit)
            def _(k=k, pairs=pairs, pair_sems=pair_sems, tiles_ref=tiles_ref):
                for n, (place, buffer) in enumerate(pairs):
                    pltpu.make_async_copy(place, buffer, pair_sems.at[n]).wait()
                up_buffer[k] += tiles_ref[k, :, :ff_shard].astype(jnp.float32)
                down_buffer[k] += tiles_ref[k, :, ff_shard:].astype(jnp.float32)
                for n, (place, buffer) in enumerate(pairs):
                    pltpu.make_async_copy(buffer, place, pair_sems.at[n]).start()

        for hit, pairs, pair_sems in copies:

            @pl.when(hit)
            def _(pairs=pairs, pair_sems=pair_sems):
                for n, (place, buffer) in enumerate(pairs):
                    pltpu.make_async_copy(buffer, place, pair_sems.at[n]).wait()


def add_in_slots(groups, slots, grad_up, grad_down):
    tile_count, rank, columns = groups[0].shape
    ff_shard = grad_up.shape[2]
    in_hbm = pl.BlockSpec(memory_space=pl.ANY)
    whole = pl.BlockSpec((tile_count, rank, columns), lambda i, s: (0, 0, 0))
    return pl.pallas_call(
        add_kernel,
        grid_spec=pltpu.PrefetchScalarGridSpec(
            num_scalar_prefetch=1,
            grid=(1,),
            in_specs=[whole] * len(groups) + [in_hbm, in_hbm],
            out_specs=[in_hbm, in_hbm],
            scratch_shapes=[
                pltpu.VMEM((tile_count, rank, ff_shard), jnp.float32),
                pltpu.VMEM((tile_count, rank, columns - ff_shard), jnp.float32),
                pltpu.SemaphoreType.DMA((tile_count, 2)),
            ],
        ),
        out_shape=[
            jax.ShapeDtypeStruct(grad_up.shape, grad_up.dtype),
            jax.ShapeDtypeStruct(grad_down.shape, grad_down.dtype),
        ],
        input_output_aliases={len(groups) + 1: 0, len(groups) + 2: 1},
        compiler_params=pltpu.CompilerParams(vmem_limit_bytes=20 * 1024 * 1024),
        cost_estimate=pl.CostEstimate(
            flops=0, bytes_accessed=4 * tile_count * rank * columns, transcendentals=0
        ),
    )(slots, *groups, grad_up, grad_down)


def terms_kernel(group_count, out_count, place_ref, *refs):
    dy_refs, refs = refs[:group_count], refs[group_count:]
    *refs, dy_buffer, weight_buffer, total, dy_sems, weight_sems = refs
    weight_refs, out_refs = refs[:-out_count], refs[-out_count:]
    chip, core = place_ref[0], place_ref[1]
    rows_group, depth = dy_refs[0].shape
    step_depth = dy_buffer.shape[-1]
    steps = depth // step_depth
    columns = total.shape[1]

    def start(step):
        slot = lax.rem(step, 2)
        part = pl.ds(pl.multiple_of(step * step_depth, step_depth), step_depth)
        for refs, buffer, sems in (
            (dy_refs, dy_buffer, dy_sems),
            (weight_refs, weight_buffer, weight_sems),
        ):
            row = 0
            for ref in refs:
                rows = pl.ds(row, ref.shape[0])
                pltpu.make_async_copy(
                    ref.at[:, part], buffer.at[slot, rows], sems.at[slot]
                ).start()
                row += ref.shape[0]

    def one_step(step, carry):
        slot = lax.rem(step, 2)

        @pl.when(step + 1 < steps)
        def _():
            start(step + 1)

        for buffer, sems in ((dy_buffer, dy_sems), (weight_buffer, weight_sems)):
            whole = buffer.at[slot]
            pltpu.make_async_copy(whole, whole, sems.at[slot]).wait()
        for column in range(0, columns, 256):
            part = dot_last(dy_buffer[slot], weight_buffer[slot, column : column + 256])
            total[:, column : column + 256] += part
        return carry

    start(jnp.int32(0))
    total[...] = jnp.zeros_like(total)
    lax.fori_loop(0, steps, one_step, 0)
    for group in range(group_count):
        for k in range(4):
            first = group * rows_group + k * TILE

            def tile(first=first):
                return total[first : first + TILE].astype(jnp.bfloat16)

            if out_count == 1:
                out_refs[0][k, group] = tile()
                continue
            x, c = k // 2, k % 2
            slot = jnp.where(chip == x, 1, 0)

            @pl.when(core != c)
            def _(slot=slot, group=group, tile=tile):
                out_refs[0][slot, group] = tile()

            @pl.when(core == c)
            def _(slot=slot, group=group, tile=tile):
                out_refs[1][slot, group] = tile()


def product_terms(groups, weights, place, out_count):
    rows_group, depth = groups[0].shape
    columns = sum(w.shape[0] for w in weights)
    rows = rows_group * len(groups)
    step_depth = 896 if depth % 896 == 0 else depth
    out = jax.ShapeDtypeStruct((4 // out_count, len(groups), TILE, columns), jnp.bfloat16)
    in_hbm = pl.BlockSpec(memory_space=pl.ANY)
    return pl.pallas_call(
        functools.partial(terms_kernel, len(groups), out_count),
        grid_spec=pltpu.PrefetchScalarGridSpec(
            num_scalar_prefetch=1,
            grid=(1,),
            in_specs=[in_hbm] * (len(groups) + len(weights)),
            out_specs=[pl.BlockSpec(out.shape, lambda i, p: (0, 0, 0, 0))] * out_count,
            scratch_shapes=[
                pltpu.VMEM((2, rows, step_depth), jnp.bfloat16),
                pltpu.VMEM((2, columns, step_depth), jnp.bfloat16),
                pltpu.VMEM((rows, columns), jnp.float32),
                pltpu.SemaphoreType.DMA((2,)),
                pltpu.SemaphoreType.DMA((2,)),
            ],
        ),
        out_shape=[out] * out_count,
        compiler_params=pltpu.CompilerParams(vmem_limit_bytes=20 * 1024 * 1024),
        cost_estimate=pl.CostEstimate(flops=0, bytes_accessed=0, transcendentals=0),
    )(place, *groups, *weights)


def assemble_kernel(flags_ref, *refs):
    own_ref, partner_ref, here_ref, out_ref, swapped_ref, diagonal_ref = refs[:6]
    backed_ref, down_ref, input_grad_ref, lora = refs[6:]
    z, rep = flags_ref[0], flags_ref[1]
    width = own_ref.shape[1]
    half = width // 2
    lora[...] = adapter_scale * lax.dot_general(
        backed_ref[...],
        down_ref[...],
        (((0,), (0,)), ((), ())),
        preferred_element_type=jnp.float32,
    )
    inner = (z == 1) | (z == 2)
    near_block = jnp.where(z < 2, 2, 1)
    far_block = jnp.where(z < 2, 3, 0)

    def put(start, values):
        columns = pl.ds(pl.multiple_of(start, half), values.shape[1])
        input_grad_ref[:, columns] = (values.astype(jnp.float32) + lora[:, columns]).astype(
            input_grad_ref.dtype
        )

    put(z * width, own_ref[...])
    put((z + 1 - 2 * lax.rem(z, 2)) * width, partner_ref[...])
    for block, columns in ((near_block, slice(0, half)), (far_block, slice(half, width))):
        mine = jnp.where(inner, here_ref[:, columns], out_ref[:, columns])
        put(block * width + rep * half, mine)
        other = jnp.where(inner, swapped_ref[:, columns], diagonal_ref[:, columns])
        put(block * width + (1 - rep) * half, other)


def assemble(z, rep, blocks, backed, own_down):
    whole = [pl.BlockSpec(x.shape, lambda i, f: (0, 0)) for x in (*blocks, backed, own_down)]
    shape = (blocks[0].shape[0], own_down.shape[1])
    return pl.pallas_call(
        assemble_kernel,
        grid_spec=pltpu.PrefetchScalarGridSpec(
            num_scalar_prefetch=1,
            grid=(1,),
            in_specs=whole,
            out_specs=pl.BlockSpec(shape, lambda i, f: (0, 0)),
            scratch_shapes=[pltpu.VMEM(shape, jnp.float32)],
        ),
        out_shape=jax.ShapeDtypeStruct(shape, jnp.bfloat16),
        compiler_params=pltpu.CompilerParams(vmem_limit_bytes=20 * 1024 * 1024),
        cost_estimate=pl.CostEstimate(flops=0, bytes_accessed=0, transcendentals=0),
    )(jnp.stack([z, rep]).astype(jnp.int32), *blocks, backed, own_down)


def after(value, *events):
    return lax.optimization_barrier((value,) + events)[0]


def from_other_core(away):
    return lax.ppermute(away, "tensor", [(0, 1), (1, 0), (2, 3), (3, 2)])


def sum_of_chips(home, got, *events):
    pair = home.astype(jnp.float32) + got.astype(jnp.float32)
    sent = after(pair[0].astype(jnp.bfloat16), *events)
    got = lax.ppermute(sent, "tensor", [(0, 2), (2, 0), (1, 3), (3, 1)])
    return (pair[1] + got.astype(jnp.float32)).astype(jnp.bfloat16)


def sum_by_swap(terms):
    got = lax.all_to_all(terms[0], "tensor", split_axis=0, concat_axis=0, tiled=True)
    return jnp.sum(got.astype(jnp.float32), axis=0).astype(jnp.bfloat16)


PARTNER = [(0, 1), (1, 0), (2, 3), (3, 2)]
MIDDLE = [(1, 2), (2, 1)]
OUTER_TO_MIDDLE = [(0, 2), (3, 1)]
OUTWARD = [(1, 0), (2, 3)]
OTHER_REP = [(0, 1), (1, 0)]
OUTWARD_OTHER_REP = [(4 * r + a, 4 * (1 - r) + b) for r in (0, 1) for a, b in OUTWARD]


def line_of_four(
    tokens,
    grad_out,
    frozen_weight,
    adapter_down,
    adapter_up,
    tenant_ids,
    tenant_token_counts,
    owner_map,
):
    z = lax.axis_index("dp")
    rep = lax.axis_index("rep")
    shard = lax.axis_index("tensor")
    place = jnp.stack([shard // 2, shard % 2]).astype(jnp.int32)
    rows_group, ff_shard = grad_out.shape
    tile_count = rows_group // TILE
    adapter_count, rank = adapter_down.shape[:2]
    slot_count = 2 * adapter_count // 4
    inner = (z == 1) | (z == 2)
    all_tenants = tenant_ids.reshape(-1, TILE)[:, 0]
    tenants = lax.dynamic_slice_in_dim(all_tenants, z * tile_count, tile_count)
    half = frozen_weight.shape[0] // 2

    def rows_of_half(start, count, *events):
        first = rep * half + start
        if events:
            first = after(first, *events)
        return lax.dynamic_slice_in_dim(frozen_weight, first, count, 0)

    quarter = half // 2
    early_rows = rows_of_half(0, quarter)
    late_rows = rows_of_half(quarter, quarter, early_rows)
    near = [lax.ppermute(early_rows, "dp", MIDDLE), lax.ppermute(late_rows, "dp", MIDDLE)]
    partner_dy = lax.ppermute(grad_out, "dp", PARTNER)

    dy_tiles = grad_out.reshape(tile_count, TILE, ff_shard)
    down_sel = adapter_down[after(tenants, late_rows)]
    other_dy = lax.ppermute(after(grad_out, down_sel), "rep", OTHER_REP)
    up_sel = adapter_up[tenants]
    own_down = lax.all_to_all(down_sel, "tensor", split_axis=0, concat_axis=2, tiled=True)[0]
    middle = dot_last(own_down, tokens).astype(jnp.bfloat16)
    backed_part = jnp.einsum(
        "krf,ktf->krt", up_sel, dy_tiles, preferred_element_type=jnp.float32
    ).astype(jnp.bfloat16)
    sent = jnp.concatenate([backed_part, jnp.broadcast_to(middle, backed_part.shape)], axis=1)
    got = lax.all_to_all(sent, "tensor", split_axis=0, concat_axis=0, tiled=True)
    backed = jnp.sum(got[:, :rank].astype(jnp.float32), axis=0).astype(jnp.bfloat16)
    middle = got[:, rank:]

    def scale_of(tenants):
        return adapter_scale / tenant_token_counts[tenants].astype(jnp.float32)

    def up_gradients(scale, middle, dy):
        dy = dy.reshape(tile_count, TILE, ff_shard)
        product = jnp.einsum("krt,ktf->krf", middle, dy, preferred_element_type=jnp.float32)
        return (scale[:, None, None] * product).astype(jnp.bfloat16)

    scale = scale_of(tenants)
    tile_up = up_gradients(scale, middle, grad_out)
    own_tile_down = (
        scale[shard] * jnp.dot(backed, tokens, preferred_element_type=jnp.float32)
    ).astype(jnp.bfloat16)
    tile_down = lax.all_to_all(
        own_tile_down, "tensor", split_axis=1, concat_axis=0, tiled=True
    ).reshape(tile_count, rank, -1)
    tile_grads = jnp.concatenate([tile_up, tile_down], axis=2)
    to_partner = jnp.concatenate([middle, tile_down], axis=2)

    from_partner = lax.ppermute(to_partner, "dp", PARTNER)

    partner_index = z + 1 - 2 * (z % 2)
    partner_tenants = lax.dynamic_slice_in_dim(
        all_tenants, partner_index * tile_count, tile_count
    )
    partner_up = up_gradients(
        scale_of(partner_tenants), from_partner[:, :, :TILE], partner_dy
    )
    partner_grads = jnp.concatenate([partner_up, from_partner[:, :, TILE:]], axis=2)
    far_rows = rows_of_half(0, half, late_rows, down_sel)
    far = lax.ppermute(after(far_rows, from_partner, partner_dy), "dp", OUTER_TO_MIDDLE)
    partner_other_dy = lax.ppermute(partner_dy, "rep", OTHER_REP)

    events = (partner_dy, tile_grads, partner_grads)
    own_terms = product_terms([after(grad_out, *events), partner_dy], [frozen_weight], place, 1)
    own_sum = sum_by_swap(own_terms)

    groups = [after(grad_out, *near, own_terms[0]), partner_dy, other_dy]
    near_terms = product_terms(groups, near, place, 1)
    near_sum = sum_by_swap(near_terms)

    near_grads = lax.ppermute(after(tile_grads, near_terms[0]), "dp", MIDDLE)
    far_grads = lax.ppermute(after(partner_grads, own_sum), "dp", MIDDLE)
    partner_block = lax.ppermute(own_sum[1], "dp", PARTNER)

    tile_slots = owner_slots(owner_map, slot_count)[all_tenants].reshape(4, tile_count)
    tile_slots = tile_slots - z * slot_count
    grad_up, grad_down = place_in_slots(
        [after(tile_grads, near_terms[0]), partner_grads],
        jnp.concatenate([tile_slots[z], tile_slots[partner_index]]),
        slot_count,
        ff_shard,
    )

    groups = [after(grad_out, own_sum, near_sum, grad_up, grad_down), partner_dy, other_dy]
    far_terms = product_terms(groups, [far], place, 2)
    outer_terms = product_terms(
        [after(partner_other_dy, far_terms[0], near_grads, partner_block)], near + [far], place, 2
    )
    near_grads_out = lax.ppermute(after(near_grads, far_terms[0]), "dp", OUTWARD)
    outer_got = from_other_core(after(outer_terms[0], far_grads))
    far_grads_out = lax.ppermute(far_grads, "dp", OUTWARD)
    far_got = from_other_core(far_terms[0])
    far_sum = sum_of_chips(far_terms[1], far_got)
    outer_sum = sum_of_chips(after(outer_terms[1], near_grads_out), outer_got)[0]
    both_sum = jnp.concatenate([near_sum, far_sum], axis=2)
    both_out = lax.ppermute(both_sum[1], "dp", OUTWARD)
    both_other = lax.ppermute(both_sum[2], "rep", OTHER_REP)
    outer_other = lax.ppermute(
        after(outer_sum, far_grads_out), ("rep", "dp"), OUTWARD_OTHER_REP
    )

    blocks = [own_sum[0], partner_block, both_sum[0], both_out, both_other, outer_other]
    input_grad = assemble(z, rep, blocks, backed, own_down)

    near_index = jnp.where(z < 2, 2, 1)
    far_index = jnp.where(z < 2, 3, 0)
    nowhere = jnp.full((tile_count,), -1, jnp.int32)
    slots = jnp.concatenate(
        [
            jnp.where(inner, tile_slots[near_index], nowhere),
            jnp.where(inner, nowhere, tile_slots[near_index]),
            jnp.where(inner, tile_slots[far_index], nowhere),
            jnp.where(inner, nowhere, tile_slots[far_index]),
        ]
    )
    grad_up, grad_down = add_in_slots(
        [near_grads, near_grads_out, far_grads, far_grads_out], slots, grad_up, grad_down
    )
    return input_grad, grad_down, grad_up


def any_line(
    tokens,
    grad_out,
    frozen_weight,
    adapter_down,
    adapter_up,
    tenant_ids,
    tenant_token_counts,
    owner_map,
):
    dp_count = lax.axis_size("dp")
    group_index = lax.axis_index("dp")
    shard_index = lax.axis_index("tensor")
    rows_group, ff_shard = grad_out.shape
    width_shard = adapter_down.shape[2]
    adapter_count = adapter_down.shape[0]
    tile_count = rows_group // TILE
    slot_count = 2 * adapter_count // dp_count
    all_tenants = tenant_ids.reshape(-1, TILE)[:, 0]
    tenants = lax.dynamic_slice_in_dim(all_tenants, group_index * tile_count, tile_count)
    columns = lax.all_to_all(tokens, "tensor", split_axis=1, concat_axis=0, tiled=True)
    down_sel = adapter_down[tenants]
    up_sel = adapter_up[tenants]
    x_tiles = columns.reshape(tile_count, TILE, width_shard)
    dy_tiles = grad_out.reshape(tile_count, TILE, ff_shard)
    middle_part = jnp.einsum("krd,ktd->krt", down_sel, x_tiles, preferred_element_type=jnp.float32)
    backed_part = jnp.einsum("krf,ktf->krt", up_sel, dy_tiles, preferred_element_type=jnp.float32)
    middle = lax.psum(middle_part.astype(jnp.bfloat16), "tensor")
    backed = lax.psum(backed_part.astype(jnp.bfloat16), "tensor")
    whole = lax.all_gather(frozen_weight, "dp", axis=0, tiled=True)
    frozen = dot_last(grad_out, whole).astype(jnp.bfloat16).astype(jnp.float32)
    lora = adapter_scale * jnp.einsum(
        "krt,krd->ktd", backed, down_sel, preferred_element_type=jnp.float32
    ).reshape(rows_group, width_shard)
    start = shard_index * width_shard
    block = lax.dynamic_slice_in_dim(frozen, start, width_shard, 1) + lora
    terms = lax.dynamic_update_slice_in_dim(frozen, block, start, 1).astype(jnp.bfloat16)
    input_grad = lax.psum_scatter(terms, "tensor", scatter_dimension=0, tiled=True)
    scale = (adapter_scale / tenant_token_counts[tenants].astype(jnp.float32))[:, None, None]
    tile_up = scale * jnp.einsum(
        "krt,ktf->krf", middle, dy_tiles, preferred_element_type=jnp.float32
    )
    tile_down = scale * jnp.einsum(
        "krt,ktd->krd", backed, x_tiles, preferred_element_type=jnp.float32
    )
    tile_grads = jnp.concatenate([tile_up, tile_down], axis=2).astype(jnp.bfloat16)
    all_grads = lax.all_gather(tile_grads, "dp", axis=0, tiled=True)
    slots = owner_slots(owner_map, slot_count)[all_tenants] - group_index * slot_count
    grad_up, grad_down = place_in_slots([all_grads], slots, slot_count, ff_shard)
    return input_grad, grad_down, grad_up


def solution(mesh):
    sizes = mesh.shape
    four = sizes["dp"] == 4 and sizes["tensor"] == 4 and sizes["rep"] == 2
    placed = (
        P(("rep", "dp", "tensor"), None),
        P(("rep", "dp"), "tensor"),
        P("dp", "tensor"),
        P("rep", None, "tensor"),
        P("rep", None, "tensor"),
        P("rep"),
        P("rep"),
        P(),
    )
    return jax.shard_map(
        line_of_four if four else any_line,
        mesh=mesh,
        in_specs=placed,
        out_specs=(
            P(("rep", "dp", "tensor"), None),
            P(("rep", "dp"), None, "tensor"),
            P(("rep", "dp"), None, "tensor"),
        ),
        check_vma=False,
    )
```
